32 devices in a mesh: clip: 2 (over x), bank: 16 (over z, y, core).
Axes of the slice: x: 2, y: 2, z: 4, core: 2. Of those that a mesh axis runs over, the one named last changes fastest.
Arguments:
- queries: bfloat16 [2, 256, 1536], P('clip', 'bank'), may hold values from -120 to 120
- keys: bfloat16 [2, 2048, 1536], P('clip', 'bank'), may hold values from -6 to 6
- values: bfloat16 [2, 2048, 1536], P('clip', 'bank'), may hold values from -6 to 6
- grad_out: bfloat16 [2, 256, 1536], P('clip', 'bank'), may hold values from -6 to 6
- null_key: bfloat16 [1536], replicated, may hold values from -4 to 4
- null_value: bfloat16 [1536], replicated, may hold values from -4 to 4
- bank_counts: int32 [2], P('clip'), may hold values from 128 to 2048, as said below
- block_slot: int32 [2, 16], P('clip', 'bank'), may hold values from 0 to 15, each once within a row
Outputs:
- grad_queries: bfloat16 [2, 256, 1536], P('clip', 'bank')
- grad_keys: bfloat16 [2, 2048, 1536], P('clip', 'bank')
- grad_values: bfloat16 [2, 2048, 1536], P('clip', 'bank')
- grad_null_key: float32 [1536], replicated
- grad_null_value: float32 [1536], replicated
The draws below stay inside these ranges and needn't reach their ends.
Inputs may be any that keep to these rules, and one draw needn't show every extreme that they name: `bank_counts`: a multiple of 128; exactly one group holds 2048 live tokens. `block_slot`: each row is a permutation of the device indices.
All inputs are finite; a program needn't handle non-finite values.
Results may differ from the reference program's by a relative error of at most 0.01155.
Values may be sent and summed in bfloat16 or wider, within the bound.
A program may use at most 64 MiB of HBM per device.

```python
import jax
import jax.numpy as jnp
from jax import lax

HEADS = 12
HD = 128
QTOK = 256
BLK = 128
HW = 1536
CLIPS = 2
BANK = 2048
N_BANK = 16


def pair_base(key):
    query_key = jax.random.fold_in(key, 101)
    bank_key = jax.random.fold_in(key, 102)
    query_base = jnp.clip(jax.random.normal(query_key, (CLIPS, QTOK, HW), jnp.float32), -6.0, 6.0)
    bank_base = jnp.clip(jax.random.normal(bank_key, (CLIPS, BANK, HW), jnp.float32), -6.0, 6.0)
    return (query_base, bank_base)


def draw_keys(key, part):
    query_base, bank_base = pair_base(key)
    return bank_base.astype(jnp.bfloat16)


def draw_queries(key, part):
    query_base, bank_base = pair_base(key)
    return query_base.astype(jnp.bfloat16)


def draw_bank_counts(key, part):
    key = jax.random.fold_in(key, 7)
    first_key, second_key = jax.random.split(key)
    busiest = jax.random.randint(first_key, (), 0, CLIPS)
    others = jax.random.randint(second_key, (CLIPS,), 1, BANK // 256 + 1)
    units = jnp.where(jnp.arange(CLIPS) == busiest, BANK // 128, others)
    return (units * 128).astype(jnp.int32)


def steps_of(key, extent, shards, low, top_value):
    factor_of, own = 1.0, jax.random.fold_in(key, 6)
    for axis_at, shards_of in shards:
        heights = jnp.exp(jax.random.uniform(jax.random.fold_in(own, axis_at), (shards_of,), jnp.float32, low / len(shards), top_value / len(shards)))
        factor_of = factor_of * jnp.repeat(heights, extent[axis_at] // shards_of).reshape([-1 if axis == axis_at else 1 for axis in range(len(extent))])
    return factor_of


def scatter_about(rng, extent, deviation, reach, shards=(), kind=jnp.bfloat16):
    factor_of = steps_of(rng, extent, shards, -0.22, 0.18) if shards else 1.0
    result = jax.random.normal(rng, extent, jnp.float32) * deviation * factor_of
    return jnp.minimum(jnp.maximum(result, -reach), reach).astype(kind)


def setup_inputs(seed: int = 0) -> dict:
    streams_of = jax.random.split(jax.random.key(seed), 9)
    queries = draw_queries(jax.random.fold_in(streams_of[8], 71), 0)
    keys = draw_keys(jax.random.fold_in(streams_of[8], 71), 0)
    values = scatter_about(streams_of[2], (CLIPS, BANK, HW), 1.0, 6.0, ((0, 2), (1, 16)))
    grad_out = scatter_about(streams_of[3], (CLIPS, QTOK, HW), 1.0, 6.0, ((0, 2), (1, 16)))
    null_key = scatter_about(streams_of[4], (HW,), 1.0, 4.0)
    null_value = scatter_about(streams_of[5], (HW,), 1.0, 4.0)
    bank_counts = draw_bank_counts(jax.random.fold_in(streams_of[8], 71), 0)
    block_slot = jax.vmap(lambda own: jax.random.permutation(own, N_BANK))(jax.random.split(streams_of[7], CLIPS)).reshape((CLIPS, N_BANK)).astype(jnp.int32)
    return dict(queries=queries, keys=keys, values=values, grad_out=grad_out, null_key=null_key, null_value=null_value, bank_counts=bank_counts, block_slot=block_slot)


def head_terms(pieces, live_keys):
    q_head, do_head, k_head, v_head, nk_head, nv_head = pieces
    score_scale = HD ** -0.5
    live_float = live_keys.astype(jnp.float32)
    scores = jnp.dot(q_head, k_head.T, preferred_element_type=jnp.float32) * score_scale
    scores = jnp.where(live_keys[None, :], scores, -1e30)
    null_score = jnp.dot(q_head, nk_head, preferred_element_type=jnp.float32) * score_scale
    row_top = jnp.maximum(jnp.max(scores, axis=1), null_score)
    totals = jnp.sum(jnp.exp(scores - row_top[:, None]) * live_float[None, :], axis=1) + jnp.exp(null_score - row_top)
    log_total = row_top + jnp.log(totals)
    probs = jnp.exp(scores - log_total[:, None]) * live_float[None, :]
    null_prob = jnp.exp(null_score - log_total)
    dprobs = jnp.dot(do_head, v_head.T, preferred_element_type=jnp.float32)
    null_dp = jnp.dot(do_head, nv_head, preferred_element_type=jnp.float32)
    row_delta = jnp.sum(probs * dprobs, axis=1) + null_prob * null_dp
    dscore = (probs * (dprobs - row_delta[:, None])).astype(jnp.bfloat16)
    null_ds = null_prob * (null_dp - row_delta)
    grad_q = (jnp.dot(dscore, k_head, preferred_element_type=jnp.float32) * score_scale
              + null_ds[:, None] * nk_head.astype(jnp.float32)[None, :] * score_scale).astype(jnp.bfloat16)
    grad_k = (jnp.dot(dscore.T, q_head, preferred_element_type=jnp.float32) * score_scale).astype(jnp.bfloat16)
    grad_v = jnp.dot(probs.astype(jnp.bfloat16).T, do_head, preferred_element_type=jnp.float32).astype(jnp.bfloat16)
    grad_nk = jnp.sum(null_ds[:, None] * q_head.astype(jnp.float32), axis=0) * score_scale
    grad_nv = jnp.sum(null_prob[:, None] * do_head.astype(jnp.float32), axis=0)
    return grad_q, grad_k, grad_v, grad_nk, grad_nv


def split_heads(matrix):
    return matrix.reshape(matrix.shape[0], HEADS, HD).transpose(1, 0, 2)


def join_heads(stacked):
    return stacked.transpose(1, 0, 2).reshape(stacked.shape[1], HEADS * HD)


def reference(queries, keys, values, grad_out, null_key, null_value, bank_counts, block_slot):
    nk_heads = null_key.reshape(HEADS, HD)
    nv_heads = null_value.reshape(HEADS, HD)

    def group_terms(pieces):
        q_group, k_group, v_group, do_group, count, slots = pieces
        positions = jnp.arange(BANK, dtype=jnp.int32)
        owner = positions // BLK
        logical = slots[owner] * BLK + positions % BLK
        live_keys = logical < count

        def one_head(items):
            return head_terms(items, live_keys)

        grad_q, grad_k, grad_v, grad_nk, grad_nv = lax.map(
            one_head, (split_heads(q_group), split_heads(do_group), split_heads(k_group), split_heads(v_group), nk_heads, nv_heads))
        return join_heads(grad_q), join_heads(grad_k), join_heads(grad_v), grad_nk.reshape(-1), grad_nv.reshape(-1)

    grad_q, grad_k, grad_v, grad_nk, grad_nv = lax.map(
        group_terms, (queries, keys, values, grad_out, bank_counts, block_slot))
    return grad_q, grad_k, grad_v, jnp.sum(grad_nk, axis=0), jnp.sum(grad_nv, axis=0)
```

```python
import functools

import jax
import jax.numpy as jnp
from jax import lax
from jax.experimental import pallas as pl
from jax.experimental.pallas import tpu as pltpu
from jax.sharding import PartitionSpec as P

HEADS = 12
HD = 128
HW = HEADS * HD
SCALE = HD ** (-0.5)
F32 = jnp.float32
BF16 = jnp.bfloat16
NT = (((1,), (1,)), ((), ()))
TN = (((0,), (0,)), ((), ()))


def nt_dot(a, b):
    return lax.dot_general(a, b, NT, preferred_element_type=F32)


def halves(x):
    high = x.astype(BF16)
    return high, (x - high.astype(F32)).astype(BF16)


def merge(lses, deltas):
    top = functools.reduce(jnp.maximum, lses)
    weights = [jnp.exp(one - top) for one in lses]
    total = sum(weights[1:], weights[0])
    mixed = weights[0] * deltas[0]
    for weight, delta in zip(weights[1:], deltas[1:]):
        mixed = mixed + weight * delta
    return top + jnp.log(total), mixed / total


def kernel(
    n_clip, n_z, rows, blk,
    valid_ref, q_ref, k_ref, v_ref, do_ref, nk_ref, nv_ref,
    gq_ref, gk_ref, gv_ref, gnk_ref, gnv_ref,
    q_all, do_all, e_s, dp_s, p_s, ds_s, dq_s, dq_out, rs_c, y_out, rs_y, acc_s, z_out, rs_z,
    peak_s, st_lo, st_z, null_s, null_sums,
    g_recv, g_send_z, g_send_y, g_send_c, st_send, st_recv, rs_send, rs_recv, n_send, n_recv,
):
    n = 4 * n_z
    qt = n * rows
    clip = lax.axis_index("clip")
    bank = lax.axis_index("bank")
    core = lax.rem(bank, 2)
    y = lax.rem(bank // 2, 2)
    z = bank // 4

    def dev(z_, y_, c_):
        return (clip, (z_ * 2 + y_) * 2 + c_)

    def place(z_, y_, c_):
        return (c_ * 2 + y_) * n_z + z_

    mine = place(z, y, core)
    others_z = [lax.rem(z + j, n_z) for j in range(1, n_z)]
    lo_peers = [(y, 1 - core), (1 - y, core), (1 - y, 1 - core)]
    to_core, to_y = dev(z, y, 1 - core), dev(z, 1 - y, core)
    clip_peers = [lax.rem(clip + j, n_clip) for j in range(1, n_clip)]

    barrier = pltpu.get_barrier_semaphore()
    peers = [dev(z, a, b) for a, b in lo_peers] + [dev(o, y, core) for o in others_z]
    peers += [(o, bank) for o in clip_peers]
    for peer in peers:
        pl.semaphore_signal(barrier, inc=1, device_id=peer, device_id_type=pl.DeviceIdType.MESH)
    pl.semaphore_wait(barrier, len(peers))

    def remote(src, dst, send, recv, device):
        copy = pltpu.make_async_remote_copy(
            src_ref=src, dst_ref=dst, send_sem=send, recv_sem=recv,
            device_id=device, device_id_type=pl.DeviceIdType.MESH,
        )
        copy.start()
        return copy

    gathered = ((q_ref, q_all), (do_ref, do_all))
    sends = []

    def own_sends(a):
        src, dst = gathered[a]
        for j, o in enumerate(others_z):
            sends.append(remote(src, dst.at[mine], g_send_z.at[a, j], g_recv.at[a, mine], dev(o, y, core)))
        sends.append(remote(src, dst.at[mine], g_send_y.at[a, 0], g_recv.at[a, mine], to_y))
        sends.append(remote(src, dst.at[mine], g_send_c.at[a, 0], g_recv.at[a, mine], to_core))

    def arrived(a, at):
        dst = gathered[a][1]
        pltpu.make_async_remote_copy(
            src_ref=dst.at[at], dst_ref=dst.at[at], send_sem=g_send_z.at[a, 0], recv_sem=g_recv.at[a, at],
            device_id=to_core, device_id_type=pl.DeviceIdType.MESH,
        ).wait_recv()

    def pass_on(a, at, send, to):
        dst = gathered[a][1]
        sends.append(remote(dst.at[at], dst.at[at], send, g_recv.at[a, at], to))

    def forward(a):
        for j, o in enumerate(others_z):
            at = place(o, y, core)
            arrived(a, at)
            pass_on(a, at, g_send_y.at[a, j + 1], to_y)
            pass_on(a, at, g_send_c.at[a, j + 1], to_core)
        for j, o in enumerate([z] + others_z):
            at = place(o, 1 - y, core)
            arrived(a, at)
            pass_on(a, at, g_send_c.at[a, n_z + j], to_core)

    def from_core(a):
        for o in [z] + others_z:
            arrived(a, place(o, y, 1 - core))
        for o in [z] + others_z:
            arrived(a, place(o, 1 - y, 1 - core))

    own_sends(0)
    own_sends(1)
    q_all[mine] = q_ref[...]
    do_all[mine] = do_ref[...]
    forward(0)
    from_core(0)
    forward(1)

    live = lax.broadcasted_iota(jnp.int32, (blk, qt), 0) < valid_ref[0, 0]
    lo = core * 2 + y

    def cols(h):
        return slice(h * HD, (h + 1) * HD)

    def head_of(ref, h):
        return ref[:, :, cols(h)].reshape(qt, HD)

    totals = []
    for h in range(HEADS):
        scores = nt_dot(k_ref[:, cols(h)], head_of(q_all, h)) * SCALE
        scores = jnp.where(live, scores, -1e30)
        peak = jnp.max(scores, axis=0, keepdims=True)
        e = jnp.exp(scores - peak)
        total = jnp.sum(e, axis=0, keepdims=True)
        e_s[h] = e
        peak_s[h : h + 1, :] = peak
        st_lo[lo, h : h + 1, :] = peak + jnp.log(total)
        totals.append(total)
    from_core(1)
    for h in range(HEADS):
        dp = nt_dot(v_ref[:, cols(h)], head_of(do_all, h))
        dp_s[h] = dp
        st_lo[lo, HEADS + h : HEADS + h + 1, :] = jnp.sum(e_s[h] * dp, axis=0, keepdims=True) / totals[h]

    st = [
        remote(st_lo.at[lo], st_lo.at[lo], st_send.at[0, i], st_recv.at[0, lo], dev(z, a, b))
        for i, (a, b) in enumerate(lo_peers)
    ]
    row_of = lax.broadcasted_iota(jnp.int32, (16, HW), 0)
    col_of = lax.broadcasted_iota(jnp.int32, (16, HW), 1)
    diagonal = (col_of >= row_of * HD) & (col_of < (row_of + 1) * HD)
    nk_diag = jnp.where(diagonal, jnp.broadcast_to(nk_ref[...].astype(F32), (16, HW)), 0.0).astype(BF16)
    nv_diag = jnp.where(diagonal, jnp.broadcast_to(nv_ref[...].astype(F32), (16, HW)), 0.0).astype(BF16)
    whole_q = q_all[...].reshape(qt, HW)
    whole_do = do_all[...].reshape(qt, HW)
    null_score = (nt_dot(nk_diag, whole_q) * SCALE)[:HEADS]
    null_dp = nt_dot(nv_diag, whole_do)[:HEADS]

    def stat_arrived(stage, buf, at):
        pltpu.make_async_remote_copy(
            src_ref=buf.at[at], dst_ref=buf.at[at], send_sem=st_send.at[stage, 0], recv_sem=st_recv.at[stage, at],
            device_id=to_core, device_id_type=pl.DeviceIdType.MESH,
        ).wait_recv()

    for a, b in lo_peers:
        stat_arrived(0, st_lo, b * 2 + a)
    lse, delta = merge([st_lo[i, :HEADS] for i in range(4)], [st_lo[i, HEADS:] for i in range(4)])
    st_z[z, :HEADS, :] = lse
    st_z[z, HEADS:, :] = delta
    for j, o in enumerate(others_z):
        st.append(remote(st_z.at[z], st_z.at[z], st_send.at[1, j], st_recv.at[1, z], dev(o, y, core)))
    for o in others_z:
        stat_arrived(1, st_z, o)
    lse, delta = merge([st_z[i, :HEADS] for i in range(n_z)], [st_z[i, HEADS:] for i in range(n_z)])
    top = jnp.maximum(lse, null_score)
    log_total = top + jnp.log(jnp.exp(lse - top) + jnp.exp(null_score - top))
    null_prob = jnp.exp(null_score - log_total)
    delta = jnp.exp(lse - log_total) * delta + null_prob * null_dp
    null_ds = null_prob * (null_dp - delta)
    factor = jnp.exp(peak_s[:HEADS] - log_total)

    for h in range(HEADS):
        probs = e_s[h] * factor[h : h + 1]
        dscore = (probs * (dp_s[h] - delta[h : h + 1])).astype(BF16)
        p_s[h] = probs.astype(BF16)
        ds_s[h] = dscore
        dq = lax.dot_general(dscore, k_ref[:, cols(h)], TN, preferred_element_type=F32) * SCALE
        dq = dq.reshape(2, 2 * n_z, rows, HD)
        dq_s[:, :, :, cols(h)] = dq
        dq_out[:, :, :, cols(h)] = dq.astype(BF16)

    rs = [remote(dq_out.at[1 - core], rs_c, rs_send.at[0], rs_recv.at[0], to_core)]

    null_s[0, :HEADS, :] = null_ds
    null_s[1, :HEADS, :] = null_prob
    null_s[:, HEADS:, :] = jnp.zeros((2, 16 - HEADS, qt), F32)
    ds_high, ds_low = halves(null_s[0])
    p_high, p_low = halves(null_s[1])

    def dot(a, b):
        return jnp.dot(a, b, preferred_element_type=F32)

    sum_k = jnp.where(diagonal, dot(ds_high, whole_q) + dot(ds_low, whole_q), 0.0) * SCALE
    sum_v = jnp.where(diagonal, dot(p_high, whole_do) + dot(p_low, whole_do), 0.0)
    null_sums[clip, 0:1, :] = jnp.sum(sum_k, axis=0, keepdims=True)
    null_sums[clip, 1:2, :] = jnp.sum(sum_v, axis=0, keepdims=True)
    ns = [
        remote(null_sums.at[clip], null_sums.at[clip], n_send.at[j], n_recv.at[clip], (o, bank))
        for j, o in enumerate(clip_peers)
    ]

    own_at = lax.broadcasted_iota(jnp.int32, (rows, qt), 1) - mine * rows
    pick = (own_at == lax.broadcasted_iota(jnp.int32, (rows, qt), 0)).astype(F32).astype(BF16)
    own_high = nt_dot(pick, ds_high).astype(BF16)
    own_low = nt_dot(pick, ds_low).astype(BF16)
    null_term = (dot(own_high, nk_diag) + dot(own_low, nk_diag)) * SCALE

    rs[0].wait_recv()
    far = pl.ds((1 - y) * n_z, n_z)
    near = pl.ds(y * n_z, n_z)
    y_out[...] = (dq_s[core, far] + rs_c[far].astype(F32)).astype(BF16)
    rs.append(remote(y_out, rs_y, rs_send.at[1], rs_recv.at[1], to_y))
    acc_s[...] = dq_s[core, near] + rs_c[near].astype(F32)
    for h in range(HEADS):
        gv_ref[:, cols(h)] = dot(p_s[h], head_of(do_all, h)).astype(BF16)
    rs[1].wait_recv()
    acc = acc_s[...] + rs_y[...].astype(F32)
    acc_s[...] = acc
    z_out[...] = acc.astype(BF16)
    for j, o in enumerate(others_z):
        rs.append(remote(z_out.at[o], rs_z.at[z], rs_send.at[2 + j], rs_recv.at[2 + z], dev(o, y, core)))
    for h in range(HEADS):
        gk_ref[:, cols(h)] = (dot(ds_s[h], head_of(q_all, h)) * SCALE).astype(BF16)
    total = acc_s[z] + null_term
    for o in others_z:
        pltpu.make_async_remote_copy(
            src_ref=z_out.at[o], dst_ref=rs_z.at[o], send_sem=rs_send.at[2], recv_sem=rs_recv.at[2 + o],
            device_id=to_core, device_id_type=pl.DeviceIdType.MESH,
        ).wait_recv()
        total = total + rs_z[o].astype(F32)
    gq_ref[...] = total.astype(BF16)
    for o in clip_peers:
        pltpu.make_async_remote_copy(
            src_ref=null_sums.at[o], dst_ref=null_sums.at[o], send_sem=n_send.at[0], recv_sem=n_recv.at[o],
            device_id=to_core, device_id_type=pl.DeviceIdType.MESH,
        ).wait_recv()
    both = null_sums[0]
    for i in range(1, n_clip):
        both = both + null_sums[i]
    gnk_ref[...] = both[0:1]
    gnv_ref[...] = both[1:2]
    for copy in sends + st + rs + ns:
        copy.wait_send()


def on_device(n_clip, n_bank, queries, keys, values, grad_out, null_key, null_value, bank_counts, block_slot):
    own_rows = queries.shape[1]
    rows = -(-own_rows // 16) * 16
    blk = keys.shape[1]
    q, do = queries[0], grad_out[0]
    if rows != own_rows:
        q = jnp.pad(q, ((0, rows - own_rows), (0, 0)))
        do = jnp.pad(do, ((0, rows - own_rows), (0, 0)))
    n_z = n_bank // 4
    qt = n_bank * rows
    valid = jnp.clip(bank_counts[0] - block_slot * blk, 0, blk)
    vmem = pl.BlockSpec(memory_space=pltpu.VMEM)
    dma = pltpu.SemaphoreType.DMA
    gq, gk, gv, gnk, gnv = pl.pallas_call(
        functools.partial(kernel, n_clip, n_z, rows, blk),
        out_shape=(
            jax.ShapeDtypeStruct((rows, HW), BF16),
            jax.ShapeDtypeStruct((blk, HW), BF16),
            jax.ShapeDtypeStruct((blk, HW), BF16),
            jax.ShapeDtypeStruct((1, HW), F32),
            jax.ShapeDtypeStruct((1, HW), F32),
        ),
        in_specs=[pl.BlockSpec(memory_space=pltpu.SMEM)] + [vmem] * 6,
        out_specs=[vmem] * 5,
        scratch_shapes=[
            pltpu.VMEM((n_bank, rows, HW), BF16),
            pltpu.VMEM((n_bank, rows, HW), BF16),
            pltpu.VMEM((HEADS, blk, qt), F32),
            pltpu.VMEM((HEADS, blk, qt), F32),
            pltpu.VMEM((HEADS, blk, qt), BF16),
            pltpu.VMEM((HEADS, blk, qt), BF16),
            pltpu.VMEM((2, 2 * n_z, rows, HW), F32),
            pltpu.VMEM((2, 2 * n_z, rows, HW), BF16),
            pltpu.VMEM((2 * n_z, rows, HW), BF16),
            pltpu.VMEM((n_z, rows, HW), BF16),
            pltpu.VMEM((n_z, rows, HW), BF16),
            pltpu.VMEM((n_z, rows, HW), F32),
            pltpu.VMEM((n_z, rows, HW), BF16),
            pltpu.VMEM((n_z, rows, HW), BF16),
            pltpu.VMEM((16, qt), F32),
            pltpu.VMEM((4, 2 * HEADS, qt), F32),
            pltpu.VMEM((n_z, 2 * HEADS, qt), F32),
            pltpu.VMEM((2, 16, qt), F32),
            pltpu.VMEM((n_clip, 2, HW), F32),
            dma((2, n_bank)),
            dma((2, n_z)),
            dma((2, n_z)),
            dma((2, 2 * n_z)),
            dma((2, max(4, n_z))),
            dma((2, max(4, n_z))),
            dma((2 + n_z,)),
            dma((2 + n_z,)),
            dma((n_clip,)),
            dma((n_clip,)),
        ],
        compiler_params=pltpu.CompilerParams(
            collective_id=0, has_side_effects=True, vmem_limit_bytes=56 * 1024 * 1024
        ),
    )(valid, q, keys[0], values[0], do, null_key.reshape(1, HW), null_value.reshape(1, HW))
    return gq[None, :own_rows], gk[None], gv[None], gnk[0], gnv[0]


def solution(mesh):
    return jax.shard_map(
        functools.partial(on_device, mesh.shape["clip"], mesh.shape["bank"]),
        mesh=mesh,
        in_specs=(
            P("clip", "bank", None),
            P("clip", "bank", None),
            P("clip", "bank", None),
            P("clip", "bank", None),
            P(),
            P(),
            P("clip"),
            P("clip", "bank"),
        ),
        out_specs=(
            P("clip", "bank", None),
            P("clip", "bank", None),
            P("clip", "bank", None),
            P(),
            P(),
        ),
        check_vma=False,
    )
```

```python
import functools

import jax
import jax.numpy as jnp
from jax import lax
from jax.experimental import pallas as pl
from jax.experimental.pallas import tpu as pltpu
from jax.sharding import PartitionSpec as P

HEADS = 12
HD = 128
HW = HEADS * HD
SCALE = HD ** (-0.5)
F32 = jnp.float32
BF16 = jnp.bfloat16
PARTS = 3
PER = HEADS // PARTS
WIDE = PER * HD
NT = (((1,), (1,)), ((), ()))
TN = (((0,), (0,)), ((), ()))


def nt_dot(a, b):
    return lax.dot_general(a, b, NT, preferred_element_type=F32)


def halves(x):
    high = x.astype(BF16)
    return high, (x - high.astype(F32)).astype(BF16)


def merge(lses, deltas):
    top = functools.reduce(jnp.maximum, lses)
    weights = [jnp.exp(one - top) for one in lses]
    total = sum(weights[1:], weights[0])
    mixed = weights[0] * deltas[0]
    for weight, delta in zip(weights[1:], deltas[1:]):
        mixed = mixed + weight * delta
    return top + jnp.log(total), mixed / total


def kernel(
    n_clip, n_z, rows, blk,
    valid_ref, q_ref, k_ref, v_ref, do_ref, nk_ref, nv_ref,
    gq_ref, gk_ref, gv_ref, gn_ref,
    q_all, do_all, e_s, dp_s, p_s, ds_s, dq_s, dq_out, rs_c, y_out, rs_y, acc_s, z_out, rs_z,
    peak_s, st_lo, st_z, null_s, null_sums,
    g_recv, g_send_z, g_send_y, g_send_c, st_send, st_recv, rs_send, rs_recv, n_send, n_recv,
):
    n = 4 * n_z
    qt = n * rows
    clip = lax.axis_index("clip")
    bank = lax.axis_index("bank")
    core = lax.rem(bank, 2)
    y = lax.rem(bank // 2, 2)
    z = bank // 4

    def dev(z_, y_, c_):
        return (clip, (z_ * 2 + y_) * 2 + c_)

    def place(z_, y_, c_):
        return (c_ * 2 + y_) * n_z + z_

    mine = place(z, y, core)
    others_z = [lax.rem(z + j, n_z) for j in range(1, n_z)]
    lo_peers = [(y, 1 - core), (1 - y, core), (1 - y, 1 - core)]
    to_core, to_y = dev(z, y, 1 - core), dev(z, 1 - y, core)
    clip_peers = [lax.rem(clip + j, n_clip) for j in range(1, n_clip)]

    barrier = pltpu.get_barrier_semaphore()
    peers = [dev(z, a, b) for a, b in lo_peers] + [dev(o, y, core) for o in others_z]
    peers += [(o, bank) for o in clip_peers]
    for peer in peers:
        pl.semaphore_signal(barrier, inc=1, device_id=peer, device_id_type=pl.DeviceIdType.MESH)
    pl.semaphore_wait(barrier, len(peers))

    def remote(src, dst, send, recv, device):
        copy = pltpu.make_async_remote_copy(
            src_ref=src, dst_ref=dst, send_sem=send, recv_sem=recv,
            device_id=device, device_id_type=pl.DeviceIdType.MESH,
        )
        copy.start()
        return copy

    gathered = ((q_ref, q_all), (do_ref, do_all))
    sends = []

    def own_sends(a):
        src, dst = gathered[a]
        for j, o in enumerate(others_z):
            sends.append(remote(src, dst.at[mine], g_send_z.at[a, j], g_recv.at[a, mine], dev(o, y, core)))
        sends.append(remote(src, dst.at[mine], g_send_y.at[a, 0], g_recv.at[a, mine], to_y))
        sends.append(remote(src, dst.at[mine], g_send_c.at[a, 0], g_recv.at[a, mine], to_core))

    def arrived(a, at):
        dst = gathered[a][1]
        pltpu.make_async_remote_copy(
            src_ref=dst.at[at], dst_ref=dst.at[at], send_sem=g_send_z.at[a, 0], recv_sem=g_recv.at[a, at],
            device_id=to_core, device_id_type=pl.DeviceIdType.MESH,
        ).wait_recv()

    def pass_on(a, at, send, to):
        dst = gathered[a][1]
        sends.append(remote(dst.at[at], dst.at[at], send, g_recv.at[a, at], to))

    def forward(a, step):
        if step < n_z - 1:
            at = place(others_z[step], y, core)
            arrived(a, at)
            pass_on(a, at, g_send_y.at[a, step + 1], to_y)
            pass_on(a, at, g_send_c.at[a, step + 1], to_core)
        else:
            j = step - (n_z - 1)
            at = place(([z] + others_z)[j], 1 - y, core)
            arrived(a, at)
            pass_on(a, at, g_send_c.at[a, n_z + j], to_core)

    def from_core(a):
        for o in [z] + others_z:
            arrived(a, place(o, y, 1 - core))
        for o in [z] + others_z:
            arrived(a, place(o, 1 - y, 1 - core))

    own_sends(0)
    own_sends(1)
    q_all[mine] = q_ref[...]
    do_all[mine] = do_ref[...]
    steps = 2 * n_z - 1
    for step in range(steps):
        forward(0, step)
    from_core(0)

    live = lax.broadcasted_iota(jnp.int32, (blk, qt), 0) < valid_ref[0, 0]
    lo = core * 2 + y

    def cols(h):
        return slice(h * HD, (h + 1) * HD)

    def head_of(ref, h):
        return ref[:, :, cols(h)].reshape(qt, HD)

    totals = []
    done = 0
    for h in range(HEADS):
        until = min(steps, (steps * max(h - 1, 0) + 8) // 9)
        for step in range(done, until):
            forward(1, step)
        done = max(done, until)
        scores = nt_dot(k_ref[:, cols(h)], head_of(q_all, h)) * SCALE
        scores = jnp.where(live, scores, -1e30)
        peak = jnp.max(scores, axis=0, keepdims=True)
        e = jnp.exp(scores - peak)
        total = jnp.sum(e, axis=0, keepdims=True)
        e_s[h] = e
        peak_s[h : h + 1, :] = peak
        st_lo[lo, h : h + 1, :] = peak + jnp.log(total)
        totals.append(total)
    for step in range(done, steps):
        forward(1, step)
    from_core(1)
    for h in range(HEADS):
        dp = nt_dot(v_ref[:, cols(h)], head_of(do_all, h))
        dp_s[h] = dp
        st_lo[lo, HEADS + h : HEADS + h + 1, :] = jnp.sum(e_s[h] * dp, axis=0, keepdims=True) / totals[h]

    st = [
        remote(st_lo.at[lo], st_lo.at[lo], st_send.at[0, i], st_recv.at[0, lo], dev(z, a, b))
        for i, (a, b) in enumerate(lo_peers)
    ]
    row_of = lax.broadcasted_iota(jnp.int32, (16, HW), 0)
    col_of = lax.broadcasted_iota(jnp.int32, (16, HW), 1)
    diagonal = (col_of >= row_of * HD) & (col_of < (row_of + 1) * HD)
    nk_diag = jnp.where(diagonal, jnp.broadcast_to(nk_ref[...].astype(F32).reshape(1, HW), (16, HW)), 0.0).astype(BF16)
    nv_diag = jnp.where(diagonal, jnp.broadcast_to(nv_ref[...].astype(F32).reshape(1, HW), (16, HW)), 0.0).astype(BF16)
    whole_q = q_all[...].reshape(qt, HW)
    whole_do = do_all[...].reshape(qt, HW)
    null_score = (nt_dot(nk_diag, whole_q) * SCALE)[:HEADS]
    null_dp = nt_dot(nv_diag, whole_do)[:HEADS]

    def stat_arrived(stage, buf, at):
        pltpu.make_async_remote_copy(
            src_ref=buf.at[at], dst_ref=buf.at[at], send_sem=st_send.at[stage, 0], recv_sem=st_recv.at[stage, at],
            device_id=to_core, device_id_type=pl.DeviceIdType.MESH,
        ).wait_recv()

    for a, b in lo_peers:
        stat_arrived(0, st_lo, b * 2 + a)
    lse, delta = merge([st_lo[i, :HEADS] for i in range(4)], [st_lo[i, HEADS:] for i in range(4)])
    st_z[z, :HEADS, :] = lse
    st_z[z, HEADS:, :] = delta
    for j, o in enumerate(others_z):
        st.append(remote(st_z.at[z], st_z.at[z], st_send.at[1, j], st_recv.at[1, z], dev(o, y, core)))
    for o in others_z:
        stat_arrived(1, st_z, o)
    lse, delta = merge([st_z[i, :HEADS] for i in range(n_z)], [st_z[i, HEADS:] for i in range(n_z)])
    top = jnp.maximum(lse, null_score)
    log_total = top + jnp.log(jnp.exp(lse - top) + jnp.exp(null_score - top))
    null_prob = jnp.exp(null_score - log_total)
    delta = jnp.exp(lse - log_total) * delta + null_prob * null_dp
    null_ds = null_prob * (null_dp - delta)
    factor = jnp.exp(peak_s[:HEADS] - log_total)

    def dot(a, b):
        return jnp.dot(a, b, preferred_element_type=F32)

    rs = []
    far = pl.ds((1 - y) * n_z, n_z)
    near = pl.ds(y * n_z, n_z)

    def part_cols(part):
        return slice(part * WIDE, (part + 1) * WIDE)

    def dq_step(part):
        for i in range(PER):
            h = part * PER + i
            probs = e_s[h] * factor[h : h + 1]
            dscore = (probs * (dp_s[h] - delta[h : h + 1])).astype(BF16)
            p_s[h] = probs.astype(BF16)
            ds_s[h] = dscore
            dq = lax.dot_general(dscore, k_ref[:, cols(h)], TN, preferred_element_type=F32) * SCALE
            dq = dq.reshape(2, 2 * n_z, rows, HD)
            dq_s[part, :, :, :, cols(i)] = dq
            dq_out[part, :, :, :, cols(i)] = dq.astype(BF16)
        rs.append(
            remote(dq_out.at[part, 1 - core], rs_c.at[part], rs_send.at[part, 0], rs_recv.at[part, 0], to_core)
        )

    def landed(buf, send, recv):
        pltpu.make_async_remote_copy(
            src_ref=buf, dst_ref=buf, send_sem=send, recv_sem=recv,
            device_id=to_core, device_id_type=pl.DeviceIdType.MESH,
        ).wait_recv()

    def y_step(part):
        landed(rs_c.at[part], rs_send.at[part, 0], rs_recv.at[part, 0])
        y_out[part] = (dq_s[part, core, far] + rs_c[part, far].astype(F32)).astype(BF16)
        rs.append(remote(y_out.at[part], rs_y.at[part], rs_send.at[part, 1], rs_recv.at[part, 1], to_y))
        acc_s[part] = dq_s[part, core, near] + rs_c[part, near].astype(F32)

    def z_step(part):
        landed(rs_y.at[part], rs_send.at[part, 1], rs_recv.at[part, 1])
        acc = acc_s[part] + rs_y[part].astype(F32)
        acc_s[part] = acc
        z_out[part] = acc.astype(BF16)
        for j, o in enumerate(others_z):
            rs.append(
                remote(
                    z_out.at[part, o], rs_z.at[part, z], rs_send.at[part, 2 + j], rs_recv.at[part, 2 + z],
                    dev(o, y, core),
                )
            )

    def grad_v(h):
        gv_ref[:, cols(h)] = dot(p_s[h], head_of(do_all, h)).astype(BF16)

    def grad_k(h):
        gk_ref[:, cols(h)] = (dot(ds_s[h], head_of(q_all, h)) * SCALE).astype(BF16)

    dq_step(0)
    dq_step(1)
    y_step(0)
    dq_step(2)
    y_step(1)
    z_step(0)
    y_step(2)

    null_s[0, :HEADS, :] = null_ds
    null_s[1, :HEADS, :] = null_prob
    null_s[:, HEADS:, :] = jnp.zeros((2, 16 - HEADS, qt), F32)
    ds_high, ds_low = halves(null_s[0])
    p_high, p_low = halves(null_s[1])

    sum_k = jnp.where(diagonal, dot(ds_high, whole_q) + dot(ds_low, whole_q), 0.0) * SCALE
    sum_v = jnp.where(diagonal, dot(p_high, whole_do) + dot(p_low, whole_do), 0.0)
    null_sums[clip, 0:1, :] = jnp.sum(sum_k, axis=0, keepdims=True)
    null_sums[clip, 1:2, :] = jnp.sum(sum_v, axis=0, keepdims=True)
    ns = [
        remote(null_sums.at[clip], null_sums.at[clip], n_send.at[j], n_recv.at[clip], (o, bank))
        for j, o in enumerate(clip_peers)
    ]
    z_step(1)
    for h in range(HEADS // 2):
        grad_v(h)
    z_step(2)
    for h in range(HEADS // 2, HEADS):
        grad_v(h)

    own_at = lax.broadcasted_iota(jnp.int32, (rows, qt), 1) - mine * rows
    pick = (own_at == lax.broadcasted_iota(jnp.int32, (rows, qt), 0)).astype(F32).astype(BF16)
    own_high = nt_dot(pick, ds_high).astype(BF16)
    own_low = nt_dot(pick, ds_low).astype(BF16)
    null_term = (dot(own_high, nk_diag) + dot(own_low, nk_diag)) * SCALE
    for h in range(HEADS):
        grad_k(h)

    for part in range(PARTS):
        total = acc_s[part, z] + null_term[:, part_cols(part)]
        for o in others_z:
            landed(rs_z.at[part, o], rs_send.at[part, 2], rs_recv.at[part, 2 + o])
            total = total + rs_z[part, o].astype(F32)
        gq_ref[:, part_cols(part)] = total.astype(BF16)
    for o in clip_peers:
        landed(null_sums.at[o], n_send.at[0], n_recv.at[o])
    both = null_sums[0]
    for i in range(1, n_clip):
        both = both + null_sums[i]
    gn_ref[...] = both
    for copy in sends + st + rs + ns:
        copy.wait_send()


def write_out(gq, gk, gv, gn, gq_out, gk_out, gv_out, gnk_out, gnv_out):
    gq_out[...] = gq[...]
    gk_out[...] = gk[...]
    gv_out[...] = gv[...]
    gnk_out[...] = gn[0]
    gnv_out[...] = gn[1]


def on_device(n_clip, n_bank, queries, keys, values, grad_out, null_key, null_value, bank_counts, block_slot):
    own_rows = queries.shape[1]
    rows = -(-own_rows // 16) * 16
    blk = keys.shape[1]
    q, do = queries[0], grad_out[0]
    if rows != own_rows:
        q = jnp.pad(q, ((0, rows - own_rows), (0, 0)))
        do = jnp.pad(do, ((0, rows - own_rows), (0, 0)))
    n_z = n_bank // 4
    qt = n_bank * rows
    valid = jnp.clip(bank_counts[0] - block_slot * blk, 0, blk)
    vmem = pl.BlockSpec(memory_space=pltpu.VMEM)
    dma = pltpu.SemaphoreType.DMA
    shapes = (
        jax.ShapeDtypeStruct((rows, HW), BF16),
        jax.ShapeDtypeStruct((blk, HW), BF16),
        jax.ShapeDtypeStruct((blk, HW), BF16),
    )
    made = pl.pallas_call(
        functools.partial(kernel, n_clip, n_z, rows, blk),
        out_shape=shapes + (jax.ShapeDtypeStruct((2, HW), F32),),
        in_specs=[pl.BlockSpec(memory_space=pltpu.SMEM)] + [vmem] * 6,
        out_specs=[vmem] * 4,
        scratch_shapes=[
            pltpu.VMEM((n_bank, rows, HW), BF16),
            pltpu.VMEM((n_bank, rows, HW), BF16),
            pltpu.VMEM((HEADS, blk, qt), F32),
            pltpu.VMEM((HEADS, blk, qt), F32),
            pltpu.VMEM((HEADS, blk, qt), BF16),
            pltpu.VMEM((HEADS, blk, qt), BF16),
            pltpu.VMEM((PARTS, 2, 2 * n_z, rows, WIDE), F32),
            pltpu.VMEM((PARTS, 2, 2 * n_z, rows, WIDE), BF16),
            pltpu.VMEM((PARTS, 2 * n_z, rows, WIDE), BF16),
            pltpu.VMEM((PARTS, n_z, rows, WIDE), BF16),
            pltpu.VMEM((PARTS, n_z, rows, WIDE), BF16),
            pltpu.VMEM((PARTS, n_z, rows, WIDE), F32),
            pltpu.VMEM((PARTS, n_z, rows, WIDE), BF16),
            pltpu.VMEM((PARTS, n_z, rows, WIDE), BF16),
            pltpu.VMEM((16, qt), F32),
            pltpu.VMEM((4, 2 * HEADS, qt), F32),
            pltpu.VMEM((n_z, 2 * HEADS, qt), F32),
            pltpu.VMEM((2, 16, qt), F32),
            pltpu.VMEM((n_clip, 2, HW), F32),
            dma((2, n_bank)),
            dma((2, n_z)),
            dma((2, n_z)),
            dma((2, 2 * n_z)),
            dma((2, max(4, n_z))),
            dma((2, max(4, n_z))),
            dma((PARTS, 2 + n_z)),
            dma((PARTS, 2 + n_z)),
            dma((n_clip,)),
            dma((n_clip,)),
        ],
        compiler_params=pltpu.CompilerParams(
            collective_id=0, has_side_effects=True, vmem_limit_bytes=min(56, 12 + qt // 16) * 1024 * 1024
        ),
    )(valid, q, keys[0], values[0], do, null_key, null_value)
    vector = jax.ShapeDtypeStruct((HW,), F32)
    gq, gk, gv, gnk, gnv = pl.pallas_call(
        write_out,
        out_shape=shapes + (vector, vector),
        in_specs=[vmem] * 4,
        out_specs=[vmem] * 5,
        compiler_params=pltpu.CompilerParams(vmem_limit_bytes=16 * 1024 * 1024),
    )(*made)
    return gq[None, :own_rows], gk[None], gv[None], gnk, gnv


def solution(mesh):
    return jax.shard_map(
        functools.partial(on_device, mesh.shape["clip"], mesh.shape["bank"]),
        mesh=mesh,
        in_specs=(
            P("clip", "bank", None),
            P("clip", "bank", None),
            P("clip", "bank", None),
            P("clip", "bank", None),
            P(),
            P(),
            P("clip"),
            P("clip", "bank"),
        ),
        out_specs=(
            P("clip", "bank", None),
            P("clip", "bank", None),
            P("clip", "bank", None),
            P(),
            P(),
        ),
        check_vma=False,
    )
```

```python
import functools

import jax
import jax.numpy as jnp
from jax import lax
from jax.experimental import pallas as pl
from jax.experimental.pallas import tpu as pltpu
from jax.sharding import PartitionSpec as P

HEADS = 12
HD = 128
HW = HEADS * HD
SCALE = HD ** (-0.5)
F32 = jnp.float32
BF16 = jnp.bfloat16
PARTS = 3
PER = HEADS // PARTS
WIDE = PER * HD
NT = (((1,), (1,)), ((), ()))
TN = (((0,), (0,)), ((), ()))


def nt_dot(a, b):
    return lax.dot_general(a, b, NT, preferred_element_type=F32)


def halves(x):
    high = x.astype(BF16)
    return high, (x - high.astype(F32)).astype(BF16)


def merge(lses, deltas):
    top = functools.reduce(jnp.maximum, lses)
    weights = [jnp.exp(one - top) for one in lses]
    total = sum(weights[1:], weights[0])
    mixed = weights[0] * deltas[0]
    for weight, delta in zip(weights[1:], deltas[1:]):
        mixed = mixed + weight * delta
    return top + jnp.log(total), mixed / total


def kernel(
    n_clip, n_z, rows, blk,
    valid_ref, q_hbm, k_hbm, v_hbm, do_hbm, nk_hbm, nv_hbm,
    gq_ref, gk_ref, gv_ref, gn_ref,
    q_all, do_all, e_s, dp_s, p_s, ds_s, dq_s, dq_out, rs_c, y_out, rs_y, acc_s, z_out, rs_z,
    peak_s, st_lo, st_z, null_s, null_sums,
    k_ref, v_ref, nk_ref, nv_ref, load_sem,
    g_recv, g_send_z, g_send_y, g_send_c, st_send, st_recv, rs_send, rs_recv, n_send, n_recv,
):
    n = 4 * n_z
    qt = n * rows
    clip = lax.axis_index("clip")
    bank = lax.axis_index("bank")
    core = lax.rem(bank, 2)
    y = lax.rem(bank // 2, 2)
    z = bank // 4

    def dev(z_, y_, c_):
        return (clip, (z_ * 2 + y_) * 2 + c_)

    def place(z_, y_, c_):
        return (c_ * 2 + y_) * n_z + z_

    mine = place(z, y, core)
    others_z = [lax.rem(z + j, n_z) for j in range(1, n_z)]
    lo_peers = [(y, 1 - core), (1 - y, core), (1 - y, 1 - core)]
    to_core, to_y = dev(z, y, 1 - core), dev(z, 1 - y, core)
    clip_peers = [lax.rem(clip + j, n_clip) for j in range(1, n_clip)]

    loads = [
        pltpu.make_async_copy(src, dst, load_sem.at[i])
        for i, (src, dst) in enumerate(
            [
                (q_hbm, q_all.at[mine]), (k_hbm, k_ref), (do_hbm, do_all.at[mine]), (v_hbm, v_ref),
                (nk_hbm, nk_ref), (nv_hbm, nv_ref),
            ]
        )
    ]
    for load in loads:
        load.start()

    barrier = pltpu.get_barrier_semaphore()
    peers = [dev(z, a, b) for a, b in lo_peers] + [dev(o, y, core) for o in others_z]
    peers += [(o, bank) for o in clip_peers]
    for peer in peers:
        pl.semaphore_signal(barrier, inc=1, device_id=peer, device_id_type=pl.DeviceIdType.MESH)
    pl.semaphore_wait(barrier, len(peers))

    def remote(src, dst, send, recv, device):
        copy = pltpu.make_async_remote_copy(
            src_ref=src, dst_ref=dst, send_sem=send, recv_sem=recv,
            device_id=device, device_id_type=pl.DeviceIdType.MESH,
        )
        copy.start()
        return copy

    half = HW // 2
    gathered = ((q_hbm, q_all, 0), (q_hbm, q_all, half), (do_hbm, do_all, 0), (do_hbm, do_all, half))
    sends = []

    def piece(a, at):
        _, dst, first = gathered[a]
        return dst.at[at, :, pl.ds(first, half)]

    def own_sends(a):
        src, _, first = gathered[a]
        src, dst = src.at[:, pl.ds(first, half)], piece(a, mine)
        for j, o in enumerate(others_z):
            sends.append(remote(src, dst, g_send_z.at[a, j], g_recv.at[a, mine], dev(o, y, core)))
        sends.append(remote(src, dst, g_send_y.at[a, 0], g_recv.at[a, mine], to_y))
        sends.append(remote(src, dst, g_send_c.at[a, 0], g_recv.at[a, mine], to_core))

    def arrived(a, at):
        pltpu.make_async_remote_copy(
            src_ref=piece(a, at), dst_ref=piece(a, at), send_sem=g_send_z.at[a, 0], recv_sem=g_recv.at[a, at],
            device_id=to_core, device_id_type=pl.DeviceIdType.MESH,
        ).wait_recv()

    def pass_on(a, at, send, to):
        sends.append(remote(piece(a, at), piece(a, at), send, g_recv.at[a, at], to))

    def forward(a, step):
        if step < n_z - 1:
            at = place(others_z[step], y, core)
            arrived(a, at)
            pass_on(a, at, g_send_y.at[a, step + 1], to_y)
            pass_on(a, at, g_send_c.at[a, step + 1], to_core)
        else:
            j = step - (n_z - 1)
            at = place(([z] + others_z)[j], 1 - y, core)
            arrived(a, at)
            pass_on(a, at, g_send_c.at[a, n_z + j], to_core)

    def from_core(a):
        for o in [z] + others_z:
            arrived(a, place(o, y, 1 - core))
        for o in [z] + others_z:
            arrived(a, place(o, 1 - y, 1 - core))

    steps = 2 * n_z - 1
    six = HEADS // 2

    def beside(a, i):
        for step in range(steps * i // six, steps * (i + 1) // six):
            forward(a, step)

    for a in range(4):
        own_sends(a)
    for step in range(steps):
        forward(0, step)
    loads[0].wait()
    loads[1].wait()
    from_core(0)

    live = lax.broadcasted_iota(jnp.int32, (blk, qt), 0) < valid_ref[0, 0]
    lo = core * 2 + y

    def cols(h):
        return slice(h * HD, (h + 1) * HD)

    def head_of(ref, h):
        return ref[:, :, cols(h)].reshape(qt, HD)

    totals = []

    def score_head(h):
        scores = nt_dot(k_ref[:, cols(h)], head_of(q_all, h)) * SCALE
        scores = jnp.where(live, scores, -1e30)
        peak = jnp.max(scores, axis=0, keepdims=True)
        e = jnp.exp(scores - peak)
        total = jnp.sum(e, axis=0, keepdims=True)
        e_s[h] = e
        peak_s[h : h + 1, :] = peak
        st_lo[lo, h : h + 1, :] = peak + jnp.log(total)
        totals.append(total)

    def delta_head(h):
        dp = nt_dot(v_ref[:, cols(h)], head_of(do_all, h))
        dp_s[h] = dp
        st_lo[lo, HEADS + h : HEADS + h + 1, :] = jnp.sum(e_s[h] * dp, axis=0, keepdims=True) / totals[h]

    for i in range(six):
        score_head(i)
        beside(1, i)
    from_core(1)
    for i in range(six):
        score_head(six + i)
        beside(2, i)
    loads[2].wait()
    loads[3].wait()
    from_core(2)
    for i in range(six):
        delta_head(i)
        beside(3, i)
    from_core(3)
    for i in range(six):
        delta_head(six + i)

    st = [
        remote(st_lo.at[lo], st_lo.at[lo], st_send.at[0, i], st_recv.at[0, lo], dev(z, a, b))
        for i, (a, b) in enumerate(lo_peers)
    ]
    loads[4].wait()
    loads[5].wait()
    row_of = lax.broadcasted_iota(jnp.int32, (16, HW), 0)
    col_of = lax.broadcasted_iota(jnp.int32, (16, HW), 1)
    diagonal = (col_of >= row_of * HD) & (col_of < (row_of + 1) * HD)
    nk_diag = jnp.where(diagonal, jnp.broadcast_to(nk_ref[...].astype(F32).reshape(1, HW), (16, HW)), 0.0).astype(BF16)
    nv_diag = jnp.where(diagonal, jnp.broadcast_to(nv_ref[...].astype(F32).reshape(1, HW), (16, HW)), 0.0).astype(BF16)
    whole_q = q_all[...].reshape(qt, HW)
    whole_do = do_all[...].reshape(qt, HW)
    null_score = (nt_dot(nk_diag, whole_q) * SCALE)[:HEADS]
    null_dp = nt_dot(nv_diag, whole_do)[:HEADS]

    def stat_arrived(stage, buf, at):
        pltpu.make_async_remote_copy(
            src_ref=buf.at[at], dst_ref=buf.at[at], send_sem=st_send.at[stage, 0], recv_sem=st_recv.at[stage, at],
            device_id=to_core, device_id_type=pl.DeviceIdType.MESH,
        ).wait_recv()

    for a, b in lo_peers:
        stat_arrived(0, st_lo, b * 2 + a)
    lse, delta = merge([st_lo[i, :HEADS] for i in range(4)], [st_lo[i, HEADS:] for i in range(4)])
    st_z[z, :HEADS, :] = lse
    st_z[z, HEADS:, :] = delta
    for j, o in enumerate(others_z):
        st.append(remote(st_z.at[z], st_z.at[z], st_send.at[1, j], st_recv.at[1, z], dev(o, y, core)))
    for o in others_z:
        stat_arrived(1, st_z, o)
    lse, delta = merge([st_z[i, :HEADS] for i in range(n_z)], [st_z[i, HEADS:] for i in range(n_z)])
    top = jnp.maximum(lse, null_score)
    log_total = top + jnp.log(jnp.exp(lse - top) + jnp.exp(null_score - top))
    null_prob = jnp.exp(null_score - log_total)
    delta = jnp.exp(lse - log_total) * delta + null_prob * null_dp
    null_ds = null_prob * (null_dp - delta)
    factor = jnp.exp(peak_s[:HEADS] - log_total)

    def dot(a, b):
        return jnp.dot(a, b, preferred_element_type=F32)

    rs = []
    far = pl.ds((1 - y) * n_z, n_z)
    near = pl.ds(y * n_z, n_z)

    def part_cols(part):
        return slice(part * WIDE, (part + 1) * WIDE)

    def dq_step(part):
        for i in range(PER):
            h = part * PER + i
            probs = e_s[h] * factor[h : h + 1]
            dscore = (probs * (dp_s[h] - delta[h : h + 1])).astype(BF16)
            p_s[h] = probs.astype(BF16)
            ds_s[h] = dscore
            dq = lax.dot_general(dscore, k_ref[:, cols(h)], TN, preferred_element_type=F32) * SCALE
            dq = dq.reshape(2, 2 * n_z, rows, HD)
            dq_s[part, :, :, :, cols(i)] = dq
            dq_out[part, :, :, :, cols(i)] = dq.astype(BF16)
        rs.append(
            remote(dq_out.at[part, 1 - core], rs_c.at[part], rs_send.at[part, 0], rs_recv.at[part, 0], to_core)
        )

    def landed(buf, send, recv):
        pltpu.make_async_remote_copy(
            src_ref=buf, dst_ref=buf, send_sem=send, recv_sem=recv,
            device_id=to_core, device_id_type=pl.DeviceIdType.MESH,
        ).wait_recv()

    def y_step(part):
        landed(rs_c.at[part], rs_send.at[part, 0], rs_recv.at[part, 0])
        y_out[part] = (dq_s[part, core, far] + rs_c[part, far].astype(F32)).astype(BF16)
        rs.append(remote(y_out.at[part], rs_y.at[part], rs_send.at[part, 1], rs_recv.at[part, 1], to_y))
        acc_s[part] = dq_s[part, core, near] + rs_c[part, near].astype(F32)

    def z_step(part):
        landed(rs_y.at[part], rs_send.at[part, 1], rs_recv.at[part, 1])
        acc = acc_s[part] + rs_y[part].astype(F32)
        acc_s[part] = acc
        z_out[part] = acc.astype(BF16)
        for j, o in enumerate(others_z):
            rs.append(
                remote(
                    z_out.at[part, o], rs_z.at[part, z], rs_send.at[part, 2 + j], rs_recv.at[part, 2 + z],
                    dev(o, y, core),
                )
            )

    def grad_v(h):
        gv_ref[:, cols(h)] = dot(p_s[h], head_of(do_all, h)).astype(BF16)

    def grad_k(h):
        gk_ref[:, cols(h)] = (dot(ds_s[h], head_of(q_all, h)) * SCALE).astype(BF16)

    dq_step(0)
    dq_step(1)
    y_step(0)
    dq_step(2)
    y_step(1)
    z_step(0)
    y_step(2)

    null_s[0, :HEADS, :] = null_ds
    null_s[1, :HEADS, :] = null_prob
    null_s[:, HEADS:, :] = jnp.zeros((2, 16 - HEADS, qt), F32)
    ds_high, ds_low = halves(null_s[0])
    p_high, p_low = halves(null_s[1])

    sum_k = jnp.where(diagonal, dot(ds_high, whole_q) + dot(ds_low, whole_q), 0.0) * SCALE
    sum_v = jnp.where(diagonal, dot(p_high, whole_do) + dot(p_low, whole_do), 0.0)
    null_sums[clip, 0:1, :] = jnp.sum(sum_k, axis=0, keepdims=True)
    null_sums[clip, 1:2, :] = jnp.sum(sum_v, axis=0, keepdims=True)
    ns = [
        remote(null_sums.at[clip], null_sums.at[clip], n_send.at[j], n_recv.at[clip], (o, bank))
        for j, o in enumerate(clip_peers)
    ]
    z_step(1)
    for h in range(HEADS // 2):
        grad_v(h)
    z_step(2)
    for h in range(HEADS // 2, HEADS):
        grad_v(h)

    own_at = lax.broadcasted_iota(jnp.int32, (rows, qt), 1) - mine * rows
    pick = (own_at == lax.broadcasted_iota(jnp.int32, (rows, qt), 0)).astype(F32).astype(BF16)
    own_high = nt_dot(pick, ds_high).astype(BF16)
    own_low = nt_dot(pick, ds_low).astype(BF16)
    null_term = (dot(own_high, nk_diag) + dot(own_low, nk_diag)) * SCALE
    for h in range(HEADS):
        grad_k(h)

    for part in range(PARTS):
        total = acc_s[part, z] + null_term[:, part_cols(part)]
        for o in others_z:
            landed(rs_z.at[part, o], rs_send.at[part, 2], rs_recv.at[part, 2 + o])
            total = total + rs_z[part, o].astype(F32)
        gq_ref[:, part_cols(part)] = total.astype(BF16)
    for o in clip_peers:
        landed(null_sums.at[o], n_send.at[0], n_recv.at[o])
    both = null_sums[0]
    for i in range(1, n_clip):
        both = both + null_sums[i]
    gn_ref[...] = both
    for copy in sends + st + rs + ns:
        copy.wait_send()


def write_out(gq, gk, gv, gn, gq_out, gk_out, gv_out, gnk_out, gnv_out):
    gq_out[...] = gq[...]
    gk_out[...] = gk[...]
    gv_out[...] = gv[...]
    gnk_out[...] = gn[0]
    gnv_out[...] = gn[1]


def on_device(n_clip, n_bank, queries, keys, values, grad_out, null_key, null_value, bank_counts, block_slot):
    own_rows = queries.shape[1]
    rows = -(-own_rows // 16) * 16
    blk = keys.shape[1]
    q, do = queries[0], grad_out[0]
    if rows != own_rows:
        q = jnp.pad(q, ((0, rows - own_rows), (0, 0)))
        do = jnp.pad(do, ((0, rows - own_rows), (0, 0)))
    n_z = n_bank // 4
    qt = n_bank * rows
    valid = jnp.clip(bank_counts[0] - block_slot * blk, 0, blk)
    vmem = pl.BlockSpec(memory_space=pltpu.VMEM)
    dma = pltpu.SemaphoreType.DMA
    shapes = (
        jax.ShapeDtypeStruct((rows, HW), BF16),
        jax.ShapeDtypeStruct((blk, HW), BF16),
        jax.ShapeDtypeStruct((blk, HW), BF16),
    )
    made = pl.pallas_call(
        functools.partial(kernel, n_clip, n_z, rows, blk),
        out_shape=shapes + (jax.ShapeDtypeStruct((2, HW), F32),),
        in_specs=[pl.BlockSpec(memory_space=pltpu.SMEM)] + [pl.BlockSpec(memory_space=pltpu.HBM)] * 6,
        out_specs=[vmem] * 4,
        scratch_shapes=[
            pltpu.VMEM((n_bank, rows, HW), BF16),
            pltpu.VMEM((n_bank, rows, HW), BF16),
            pltpu.VMEM((HEADS, blk, qt), F32),
            pltpu.VMEM((HEADS, blk, qt), F32),
            pltpu.VMEM((HEADS, blk, qt), BF16),
            pltpu.VMEM((HEADS, blk, qt), BF16),
            pltpu.VMEM((PARTS, 2, 2 * n_z, rows, WIDE), F32),
            pltpu.VMEM((PARTS, 2, 2 * n_z, rows, WIDE), BF16),
            pltpu.VMEM((PARTS, 2 * n_z, rows, WIDE), BF16),
            pltpu.VMEM((PARTS, n_z, rows, WIDE), BF16),
            pltpu.VMEM((PARTS, n_z, rows, WIDE), BF16),
            pltpu.VMEM((PARTS, n_z, rows, WIDE), F32),
            pltpu.VMEM((PARTS, n_z, rows, WIDE), BF16),
            pltpu.VMEM((PARTS, n_z, rows, WIDE), BF16),
            pltpu.VMEM((16, qt), F32),
            pltpu.VMEM((4, 2 * HEADS, qt), F32),
            pltpu.VMEM((n_z, 2 * HEADS, qt), F32),
            pltpu.VMEM((2, 16, qt), F32),
            pltpu.VMEM((n_clip, 2, HW), F32),
            pltpu.VMEM((blk, HW), BF16),
            pltpu.VMEM((blk, HW), BF16),
            pltpu.VMEM((HW,), BF16),
            pltpu.VMEM((HW,), BF16),
            dma((6,)),
            dma((4, n_bank)),
            dma((4, n_z)),
            dma((4, n_z)),
            dma((4, 2 * n_z)),
            dma((2, max(4, n_z))),
            dma((2, max(4, n_z))),
            dma((PARTS, 2 + n_z)),
            dma((PARTS, 2 + n_z)),
            dma((n_clip,)),
            dma((n_clip,)),
        ],
        compiler_params=pltpu.CompilerParams(
            collective_id=0, has_side_effects=True, vmem_limit_bytes=58 * 1024 * 1024
        ),
    )(valid, q, keys[0], values[0], do, null_key, null_value)
    vector = jax.ShapeDtypeStruct((HW,), F32)
    gq, gk, gv, gnk, gnv = pl.pallas_call(
        write_out,
        out_shape=shapes + (vector, vector),
        in_specs=[vmem] * 4,
        out_specs=[vmem] * 5,
        compiler_params=pltpu.CompilerParams(vmem_limit_bytes=16 * 1024 * 1024),
    )(*made)
    return gq[None, :own_rows], gk[None], gv[None], gnk, gnv


def solution(mesh):
    return jax.shard_map(
        functools.partial(on_device, mesh.shape["clip"], mesh.shape["bank"]),
        mesh=mesh,
        in_specs=(
            P("clip", "bank", None),
            P("clip", "bank", None),
            P("clip", "bank", None),
            P("clip", "bank", None),
            P(),
            P(),
            P("clip"),
            P("clip", "bank"),
        ),
        out_specs=(
            P("clip", "bank", None),
            P("clip", "bank", None),
            P("clip", "bank", None),
            P(),
            P(),
        ),
        check_vma=False,
    )
```

```python
import functools

import jax
import jax.numpy as jnp
from jax import lax
from jax.experimental import pallas as pl
from jax.experimental.pallas import tpu as pltpu
from jax.sharding import PartitionSpec as P

HEADS = 12
HD = 128
HW = HEADS * HD
SCALE = HD ** (-0.5)
F32 = jnp.float32
BF16 = jnp.bfloat16
PARTS = 3
PER = HEADS // PARTS
WIDE = PER * HD
NT = (((1,), (1,)), ((), ()))
TN = (((0,), (0,)), ((), ()))


def nt_dot(a, b):
    return lax.dot_general(a, b, NT, preferred_element_type=F32)


def halves(x):
    high = x.astype(BF16)
    return high, (x - high.astype(F32)).astype(BF16)


def merge(lses, deltas):
    top = functools.reduce(jnp.maximum, lses)
    weights = [jnp.exp(one - top) for one in lses]
    total = sum(weights[1:], weights[0])
    mixed = weights[0] * deltas[0]
    for weight, delta in zip(weights[1:], deltas[1:]):
        mixed = mixed + weight * delta
    return top + jnp.log(total), mixed / total


def kernel(
    n_clip, n_z, rows, blk,
    valid_ref, q_hbm, k_hbm, v_hbm, do_hbm, nk_hbm, nv_hbm,
    gq_ref, gk_hbm, gv_hbm, gn_ref,
    q_all, do_all, e_s, dp_s, p_s, ds_s, dq_s, dq_out, rs_c, y_out, rs_y, acc_s, z_out, rs_z,
    peak_s, st_lo, st_z, null_s, null_sums,
    k_ref, v_ref, nk_ref, nv_ref, gk_ref, gv_ref, load_sem,
    g_recv, g_recv_c, g_send_z, g_send_y, g_send_c, st_send, st_recv, rs_send, rs_recv, n_send, n_recv,
):
    n = 4 * n_z
    qt = n * rows
    clip = lax.axis_index("clip")
    bank = lax.axis_index("bank")
    core = lax.rem(bank, 2)
    y = lax.rem(bank // 2, 2)
    z = bank // 4

    def dev(z_, y_, c_):
        return (clip, (z_ * 2 + y_) * 2 + c_)

    def place(z_, y_, c_):
        return (c_ * 2 + y_) * n_z + z_

    mine = place(z, y, core)
    others_z = [lax.rem(z + j, n_z) for j in range(1, n_z)]
    lo_peers = [(y, 1 - core), (1 - y, core), (1 - y, 1 - core)]
    to_core, to_y = dev(z, y, 1 - core), dev(z, 1 - y, core)
    clip_peers = [lax.rem(clip + j, n_clip) for j in range(1, n_clip)]

    loads = [
        pltpu.make_async_copy(src, dst, load_sem.at[i])
        for i, (src, dst) in enumerate(
            [
                (q_hbm, q_all.at[mine]), (do_hbm, do_all.at[mine]), (k_hbm, k_ref), (v_hbm, v_ref),
                (nk_hbm, nk_ref), (nv_hbm, nv_ref),
            ]
        )
    ]
    for load in loads:
        load.start()

    barrier = pltpu.get_barrier_semaphore()
    peers = [dev(z, a, b) for a, b in lo_peers] + [dev(o, y, core) for o in others_z]
    peers += [(o, bank) for o in clip_peers]
    for peer in peers:
        pl.semaphore_signal(barrier, inc=1, device_id=peer, device_id_type=pl.DeviceIdType.MESH)
    pl.semaphore_wait(barrier, len(peers))

    def remote(src, dst, send, recv, device):
        copy = pltpu.make_async_remote_copy(
            src_ref=src, dst_ref=dst, send_sem=send, recv_sem=recv,
            device_id=device, device_id_type=pl.DeviceIdType.MESH,
        )
        copy.start()
        return copy

    gathered = (q_all, do_all)
    sends = []

    def own_sends(a):
        own = gathered[a].at[mine]
        for j, o in enumerate(others_z):
            sends.append(remote(own, own, g_send_z.at[a, j], g_recv.at[a, mine], dev(o, y, core)))
        sends.append(remote(own, own, g_send_y.at[a, 0], g_recv.at[a, mine], to_y))

    def landed(buf, send, recv):
        pltpu.make_async_remote_copy(
            src_ref=buf, dst_ref=buf, send_sem=send, recv_sem=recv,
            device_id=to_core, device_id_type=pl.DeviceIdType.MESH,
        ).wait_recv()

    def slab(a, y_, c_):
        return gathered[a].at[pl.ds(place(0, y_, c_), n_z)]

    def to_other_core(a, y_):
        here = slab(a, y_, core)
        sends.append(remote(here, here, g_send_c.at[a, y_], g_recv_c.at[a, y_], to_core))

    def forward(a, step):
        if step < n_z - 1:
            at = place(others_z[step], y, core)
            here = gathered[a].at[at]
            landed(here, g_send_z.at[a, 0], g_recv.at[a, at])
            sends.append(remote(here, here, g_send_y.at[a, step + 1], g_recv.at[a, at], to_y))
            if step == n_z - 2:
                to_other_core(a, y)
        else:
            at = place(([z] + others_z)[step - (n_z - 1)], 1 - y, core)
            landed(gathered[a].at[at], g_send_z.at[a, 0], g_recv.at[a, at])
            if step == 2 * n_z - 2:
                to_other_core(a, 1 - y)

    def from_core(a):
        for y_ in (y, 1 - y):
            landed(slab(a, y_, 1 - core), g_send_c.at[a, 0], g_recv_c.at[a, y_])

    loads[0].wait()
    own_sends(0)
    loads[1].wait()
    own_sends(1)
    steps = 2 * n_z - 1
    for step in range(steps):
        forward(0, step)
    loads[2].wait()
    from_core(0)

    live = lax.broadcasted_iota(jnp.int32, (blk, qt), 0) < valid_ref[0, 0]
    lo = core * 2 + y

    def cols(h):
        return slice(h * HD, (h + 1) * HD)

    def head_of(ref, h):
        return ref[:, :, cols(h)].reshape(qt, HD)

    totals = []
    done = 0
    for h in range(HEADS):
        until = min(steps, (steps * max(h - 1, 0) + 8) // 9)
        for step in range(done, until):
            forward(1, step)
        done = max(done, until)
        scores = nt_dot(k_ref[:, cols(h)], head_of(q_all, h)) * SCALE
        scores = jnp.where(live, scores, -1e30)
        peak = jnp.max(scores, axis=0, keepdims=True)
        e = jnp.exp(scores - peak)
        total = jnp.sum(e, axis=0, keepdims=True)
        e_s[h] = e
        peak_s[h : h + 1, :] = peak
        st_lo[lo, h : h + 1, :] = peak + jnp.log(total)
        totals.append(total)
    for step in range(done, steps):
        forward(1, step)
    loads[3].wait()
    from_core(1)
    for h in range(HEADS):
        dp = nt_dot(v_ref[:, cols(h)], head_of(do_all, h))
        dp_s[h] = dp
        st_lo[lo, HEADS + h : HEADS + h + 1, :] = jnp.sum(e_s[h] * dp, axis=0, keepdims=True) / totals[h]

    st = [
        remote(st_lo.at[lo], st_lo.at[lo], st_send.at[0, i], st_recv.at[0, lo], dev(z, a, b))
        for i, (a, b) in enumerate(lo_peers)
    ]
    loads[4].wait()
    loads[5].wait()
    row_of = lax.broadcasted_iota(jnp.int32, (16, HW), 0)
    col_of = lax.broadcasted_iota(jnp.int32, (16, HW), 1)
    diagonal = (col_of >= row_of * HD) & (col_of < (row_of + 1) * HD)
    nk_diag = jnp.where(diagonal, jnp.broadcast_to(nk_ref[...].astype(F32).reshape(1, HW), (16, HW)), 0.0).astype(BF16)
    nv_diag = jnp.where(diagonal, jnp.broadcast_to(nv_ref[...].astype(F32).reshape(1, HW), (16, HW)), 0.0).astype(BF16)
    whole_q = q_all[...].reshape(qt, HW)
    whole_do = do_all[...].reshape(qt, HW)
    null_score = (nt_dot(nk_diag, whole_q) * SCALE)[:HEADS]
    null_dp = nt_dot(nv_diag, whole_do)[:HEADS]

    def stat_arrived(stage, buf, at):
        pltpu.make_async_remote_copy(
            src_ref=buf.at[at], dst_ref=buf.at[at], send_sem=st_send.at[stage, 0], recv_sem=st_recv.at[stage, at],
            device_id=to_core, device_id_type=pl.DeviceIdType.MESH,
        ).wait_recv()

    for a, b in lo_peers:
        stat_arrived(0, st_lo, b * 2 + a)
    lse, delta = merge([st_lo[i, :HEADS] for i in range(4)], [st_lo[i, HEADS:] for i in range(4)])
    st_z[z, :HEADS, :] = lse
    st_z[z, HEADS:, :] = delta
    for j, o in enumerate(others_z):
        st.append(remote(st_z.at[z], st_z.at[z], st_send.at[1, j], st_recv.at[1, z], dev(o, y, core)))
    for o in others_z:
        stat_arrived(1, st_z, o)
    lse, delta = merge([st_z[i, :HEADS] for i in range(n_z)], [st_z[i, HEADS:] for i in range(n_z)])
    top = jnp.maximum(lse, null_score)
    log_total = top + jnp.log(jnp.exp(lse - top) + jnp.exp(null_score - top))
    null_prob = jnp.exp(null_score - log_total)
    delta = jnp.exp(lse - log_total) * delta + null_prob * null_dp
    null_ds = null_prob * (null_dp - delta)
    factor = jnp.exp(peak_s[:HEADS] - log_total)

    def dot(a, b):
        return jnp.dot(a, b, preferred_element_type=F32)

    rs = []
    far = pl.ds((1 - y) * n_z, n_z)
    near = pl.ds(y * n_z, n_z)

    def part_cols(part):
        return slice(part * WIDE, (part + 1) * WIDE)

    def dq_step(part):
        for i in range(PER):
            h = part * PER + i
            probs = e_s[h] * factor[h : h + 1]
            dscore = (probs * (dp_s[h] - delta[h : h + 1])).astype(BF16)
            p_s[h] = probs.astype(BF16)
            ds_s[h] = dscore
            dq = lax.dot_general(dscore, k_ref[:, cols(h)], TN, preferred_element_type=F32) * SCALE
            dq = dq.reshape(2, 2 * n_z, rows, HD)
            dq_s[part, :, :, :, cols(i)] = dq
            dq_out[part, :, :, :, cols(i)] = dq.astype(BF16)
        rs.append(
            remote(dq_out.at[part, 1 - core], rs_c.at[part], rs_send.at[part, 0], rs_recv.at[part, 0], to_core)
        )

    def y_step(part):
        landed(rs_c.at[part], rs_send.at[part, 0], rs_recv.at[part, 0])
        y_out[part] = (dq_s[part, core, far] + rs_c[part, far].astype(F32)).astype(BF16)
        rs.append(remote(y_out.at[part], rs_y.at[part], rs_send.at[part, 1], rs_recv.at[part, 1], to_y))
        acc_s[part] = dq_s[part, core, near] + rs_c[part, near].astype(F32)

    def z_step(part):
        landed(rs_y.at[part], rs_send.at[part, 1], rs_recv.at[part, 1])
        acc = acc_s[part] + rs_y[part].astype(F32)
        acc_s[part] = acc
        z_out[part] = acc.astype(BF16)
        for j, o in enumerate(others_z):
            rs.append(
                remote(
                    z_out.at[part, o], rs_z.at[part, z], rs_send.at[part, 2 + j], rs_recv.at[part, 2 + z],
                    dev(o, y, core),
                )
            )

    def grad_v(h):
        gv_ref[:, cols(h)] = dot(p_s[h], head_of(do_all, h)).astype(BF16)

    def grad_k(h):
        gk_ref[:, cols(h)] = (dot(ds_s[h], head_of(q_all, h)) * SCALE).astype(BF16)

    dq_step(0)
    dq_step(1)
    y_step(0)
    dq_step(2)
    y_step(1)
    z_step(0)
    y_step(2)

    null_s[0, :HEADS, :] = null_ds
    null_s[1, :HEADS, :] = null_prob
    null_s[:, HEADS:, :] = jnp.zeros((2, 16 - HEADS, qt), F32)
    ds_high, ds_low = halves(null_s[0])
    p_high, p_low = halves(null_s[1])

    sum_k = jnp.where(diagonal, dot(ds_high, whole_q) + dot(ds_low, whole_q), 0.0) * SCALE
    sum_v = jnp.where(diagonal, dot(p_high, whole_do) + dot(p_low, whole_do), 0.0)
    null_sums[clip, 0:1, :] = jnp.sum(sum_k, axis=0, keepdims=True)
    null_sums[clip, 1:2, :] = jnp.sum(sum_v, axis=0, keepdims=True)
    ns = [
        remote(null_sums.at[clip], null_sums.at[clip], n_send.at[j], n_recv.at[clip], (o, bank))
        for j, o in enumerate(clip_peers)
    ]
    z_step(1)
    for h in range(HEADS // 2):
        grad_v(h)
    z_step(2)
    for h in range(HEADS // 2, HEADS):
        grad_v(h)
    stores = [pltpu.make_async_copy(gv_ref, gv_hbm, load_sem.at[6])]
    stores[0].start()

    own_at = lax.broadcasted_iota(jnp.int32, (rows, qt), 1) - mine * rows
    pick = (own_at == lax.broadcasted_iota(jnp.int32, (rows, qt), 0)).astype(F32).astype(BF16)
    own_high = nt_dot(pick, ds_high).astype(BF16)
    own_low = nt_dot(pick, ds_low).astype(BF16)
    null_term = (dot(own_high, nk_diag) + dot(own_low, nk_diag)) * SCALE
    for h in range(HEADS):
        grad_k(h)
    stores.append(pltpu.make_async_copy(gk_ref, gk_hbm, load_sem.at[7]))
    stores[1].start()

    for part in range(PARTS):
        total = acc_s[part, z] + null_term[:, part_cols(part)]
        for o in others_z:
            landed(rs_z.at[part, o], rs_send.at[part, 2], rs_recv.at[part, 2 + o])
            total = total + rs_z[part, o].astype(F32)
        gq_ref[:, part_cols(part)] = total.astype(BF16)
    for o in clip_peers:
        landed(null_sums.at[o], n_send.at[0], n_recv.at[o])
    both = null_sums[0]
    for i in range(1, n_clip):
        both = both + null_sums[i]
    gn_ref[...] = both
    for copy in sends + st + rs + ns:
        copy.wait_send()
    for store in stores:
        store.wait()


def write_out(gq, gk, gv, gn, gq_out, gk_out, gv_out, gnk_out, gnv_out):
    gq_out[...] = gq[...]
    gk_out[...] = gk[...]
    gv_out[...] = gv[...]
    gnk_out[...] = gn[0]
    gnv_out[...] = gn[1]


def on_device(n_clip, n_bank, queries, keys, values, grad_out, null_key, null_value, bank_counts, block_slot):
    own_rows = queries.shape[1]
    rows = -(-own_rows // 16) * 16
    blk = keys.shape[1]
    q, do = queries[0], grad_out[0]
    if rows != own_rows:
        q = jnp.pad(q, ((0, rows - own_rows), (0, 0)))
        do = jnp.pad(do, ((0, rows - own_rows), (0, 0)))
    n_z = n_bank // 4
    qt = n_bank * rows
    valid = jnp.clip(bank_counts[0] - block_slot * blk, 0, blk)
    vmem = pl.BlockSpec(memory_space=pltpu.VMEM)
    hbm = pl.BlockSpec(memory_space=pltpu.HBM)
    dma = pltpu.SemaphoreType.DMA
    shapes = (
        jax.ShapeDtypeStruct((rows, HW), BF16),
        jax.ShapeDtypeStruct((blk, HW), BF16),
        jax.ShapeDtypeStruct((blk, HW), BF16),
    )
    made = pl.pallas_call(
        functools.partial(kernel, n_clip, n_z, rows, blk),
        out_shape=shapes + (jax.ShapeDtypeStruct((2, HW), F32),),
        in_specs=[pl.BlockSpec(memory_space=pltpu.SMEM)] + [hbm] * 6,
        out_specs=[vmem, hbm, hbm, vmem],
        scratch_shapes=[
            pltpu.VMEM((n_bank, rows, HW), BF16),
            pltpu.VMEM((n_bank, rows, HW), BF16),
            pltpu.VMEM((HEADS, blk, qt), F32),
            pltpu.VMEM((HEADS, blk, qt), F32),
            pltpu.VMEM((HEADS, blk, qt), BF16),
            pltpu.VMEM((HEADS, blk, qt), BF16),
            pltpu.VMEM((PARTS, 2, 2 * n_z, rows, WIDE), F32),
            pltpu.VMEM((PARTS, 2, 2 * n_z, rows, WIDE), BF16),
            pltpu.VMEM((PARTS, 2 * n_z, rows, WIDE), BF16),
            pltpu.VMEM((PARTS, n_z, rows, WIDE), BF16),
            pltpu.VMEM((PARTS, n_z, rows, WIDE), BF16),
            pltpu.VMEM((PARTS, n_z, rows, WIDE), F32),
            pltpu.VMEM((PARTS, n_z, rows, WIDE), BF16),
            pltpu.VMEM((PARTS, n_z, rows, WIDE), BF16),
            pltpu.VMEM((16, qt), F32),
            pltpu.VMEM((4, 2 * HEADS, qt), F32),
            pltpu.VMEM((n_z, 2 * HEADS, qt), F32),
            pltpu.VMEM((2, 16, qt), F32),
            pltpu.VMEM((n_clip, 2, HW), F32),
            pltpu.VMEM((blk, HW), BF16),
            pltpu.VMEM((blk, HW), BF16),
            pltpu.VMEM((HW,), BF16),
            pltpu.VMEM((HW,), BF16),
            pltpu.VMEM((blk, HW), BF16),
            pltpu.VMEM((blk, HW), BF16),
            dma((8,)),
            dma((2, n_bank)),
            dma((2, 2)),
            dma((2, n_z)),
            dma((2, n_z)),
            dma((2, 2)),
            dma((2, max(4, n_z))),
            dma((2, max(4, n_z))),
            dma((PARTS, 2 + n_z)),
            dma((PARTS, 2 + n_z)),
            dma((n_clip,)),
            dma((n_clip,)),
        ],
        compiler_params=pltpu.CompilerParams(
            collective_id=0, has_side_effects=True, vmem_limit_bytes=58 * 1024 * 1024
        ),
    )(valid, q, keys[0], values[0], do, null_key, null_value)
    vector = jax.ShapeDtypeStruct((HW,), F32)
    gq, gk, gv, gnk, gnv = pl.pallas_call(
        write_out,
        out_shape=shapes + (vector, vector),
        in_specs=[vmem] * 4,
        out_specs=[vmem] * 5,
        compiler_params=pltpu.CompilerParams(vmem_limit_bytes=60 * 1024 * 1024),
    )(*made)
    return gq[None, :own_rows], gk[None], gv[None], gnk, gnv


def solution(mesh):
    return jax.shard_map(
        functools.partial(on_device, mesh.shape["clip"], mesh.shape["bank"]),
        mesh=mesh,
        in_specs=(
            P("clip", "bank", None),
            P("clip", "bank", None),
            P("clip", "bank", None),
            P("clip", "bank", None),
            P(),
            P(),
            P("clip"),
            P("clip", "bank"),
        ),
        out_specs=(
            P("clip", "bank", None),
            P("clip", "bank", None),
            P("clip", "bank", None),
            P(),
            P(),
        ),
        check_vma=False,
    )
```

```python
import functools

import jax
import jax.numpy as jnp
from jax import lax
from jax.experimental import pallas as pl
from jax.experimental.pallas import tpu as pltpu
from jax.sharding import PartitionSpec as P

HEADS = 12
HD = 128
HW = HEADS * HD
SCALE = HD ** (-0.5)
F32 = jnp.float32
BF16 = jnp.bfloat16
PARTS = 3
PER = HEADS // PARTS
WIDE = PER * HD
NT = (((1,), (1,)), ((), ()))
TN = (((0,), (0,)), ((), ()))


def nt_dot(a, b):
    return lax.dot_general(a, b, NT, preferred_element_type=F32)


def halves(x):
    high = x.astype(BF16)
    return high, (x - high.astype(F32)).astype(BF16)


def merge(lses, deltas):
    top = functools.reduce(jnp.maximum, lses)
    weights = [jnp.exp(one - top) for one in lses]
    total = sum(weights[1:], weights[0])
    mixed = weights[0] * deltas[0]
    for weight, delta in zip(weights[1:], deltas[1:]):
        mixed = mixed + weight * delta
    return top + jnp.log(total), mixed / total


def kernel(
    n_clip, n_z, rows, blk,
    count_ref, slot_ref, q_hbm, k_hbm, v_hbm, do_hbm, nk_hbm, nv_hbm,
    gq_ref, gk_hbm, gv_hbm, gnk_ref, gnv_ref,
    q_all, do_all, e_s, dp_s, p_s, ds_s, dq_s, dq_out, rs_c, y_out, rs_y, acc_s, z_out, rs_z,
    peak_s, st_lo, st_z, null_s, null_sums,
    k_ref, v_ref, nk_ref, nv_ref, gk_ref, gv_ref, load_sem,
    g_recv, g_recv_c, g_send_z, g_send_y, g_send_c, st_send, st_recv, rs_send, rs_recv, n_send, n_recv,
):
    n = 4 * n_z
    qt = n * rows
    clip = lax.axis_index("clip")
    bank = lax.axis_index("bank")
    core = lax.rem(bank, 2)
    y = lax.rem(bank // 2, 2)
    z = bank // 4

    def dev(z_, y_, c_):
        return (clip, (z_ * 2 + y_) * 2 + c_)

    def place(z_, y_, c_):
        return (c_ * 2 + y_) * n_z + z_

    mine = place(z, y, core)
    others_z = [lax.rem(z + j, n_z) for j in range(1, n_z)]
    lo_peers = [(y, 1 - core), (1 - y, core), (1 - y, 1 - core)]
    to_core, to_y = dev(z, y, 1 - core), dev(z, 1 - y, core)
    clip_peers = [lax.rem(clip + j, n_clip) for j in range(1, n_clip)]

    loads = [
        pltpu.make_async_copy(src, dst, load_sem.at[i])
        for i, (src, dst) in enumerate(
            [
                (q_hbm, q_all.at[mine]), (do_hbm, do_all.at[mine]), (k_hbm, k_ref), (v_hbm, v_ref),
                (nk_hbm, nk_ref), (nv_hbm, nv_ref),
            ]
        )
    ]
    for load in loads:
        load.start()

    barrier = pltpu.get_barrier_semaphore()
    peers = [dev(z, a, b) for a, b in lo_peers] + [dev(o, y, core) for o in others_z]
    peers += [(o, bank) for o in clip_peers]
    for peer in peers:
        pl.semaphore_signal(barrier, inc=1, device_id=peer, device_id_type=pl.DeviceIdType.MESH)
    pl.semaphore_wait(barrier, len(peers))

    def remote(src, dst, send, recv, device):
        copy = pltpu.make_async_remote_copy(
            src_ref=src, dst_ref=dst, send_sem=send, recv_sem=recv,
            device_id=device, device_id_type=pl.DeviceIdType.MESH,
        )
        copy.start()
        return copy

    gathered = (q_all, do_all)
    sends = []

    def own_sends(a):
        own = gathered[a].at[mine]
        for j, o in enumerate(others_z):
            sends.append(remote(own, own, g_send_z.at[a, j], g_recv.at[a, mine], dev(o, y, core)))
        sends.append(remote(own, own, g_send_y.at[a, 0], g_recv.at[a, mine], to_y))

    def landed(buf, send, recv):
        pltpu.make_async_remote_copy(
            src_ref=buf, dst_ref=buf, send_sem=send, recv_sem=recv,
            device_id=to_core, device_id_type=pl.DeviceIdType.MESH,
        ).wait_recv()

    def slab(a, y_, c_):
        return gathered[a].at[pl.ds(place(0, y_, c_), n_z)]

    def to_other_core(a, y_):
        here = slab(a, y_, core)
        sends.append(remote(here, here, g_send_c.at[a, y_], g_recv_c.at[a, y_], to_core))

    def forward(a, step):
        if step < n_z - 1:
            at = place(others_z[step], y, core)
            here = gathered[a].at[at]
            landed(here, g_send_z.at[a, 0], g_recv.at[a, at])
            sends.append(remote(here, here, g_send_y.at[a, step + 1], g_recv.at[a, at], to_y))
            if step == n_z - 2:
                to_other_core(a, y)
        else:
            at = place(([z] + others_z)[step - (n_z - 1)], 1 - y, core)
            landed(gathered[a].at[at], g_send_z.at[a, 0], g_recv.at[a, at])
            if step == 2 * n_z - 2:
                to_other_core(a, 1 - y)

    def from_core(a):
        for y_ in (y, 1 - y):
            landed(slab(a, y_, 1 - core), g_send_c.at[a, 0], g_recv_c.at[a, y_])

    loads[0].wait()
    own_sends(0)
    loads[1].wait()
    own_sends(1)
    steps = 2 * n_z - 1
    for step in range(steps):
        forward(0, step)
    loads[2].wait()
    from_core(0)

    live = lax.broadcasted_iota(jnp.int32, (blk, qt), 0) < count_ref[0] - slot_ref[0, 0] * blk
    lo = core * 2 + y

    def cols(h):
        return slice(h * HD, (h + 1) * HD)

    def head_of(ref, h):
        return ref[:, :, cols(h)].reshape(qt, HD)

    totals = []
    done = 0
    for h in range(HEADS):
        until = min(steps, (steps * max(h - 1, 0) + 8) // 9)
        for step in range(done, until):
            forward(1, step)
        done = max(done, until)
        scores = nt_dot(k_ref[:, cols(h)], head_of(q_all, h)) * SCALE
        scores = jnp.where(live, scores, -1e30)
        peak = jnp.max(scores, axis=0, keepdims=True)
        e = jnp.exp(scores - peak)
        total = jnp.sum(e, axis=0, keepdims=True)
        e_s[h] = e
        peak_s[h : h + 1, :] = peak
        st_lo[lo, h : h + 1, :] = peak + jnp.log(total)
        totals.append(total)
    for step in range(done, steps):
        forward(1, step)
    loads[3].wait()
    from_core(1)
    for h in range(HEADS):
        dp = nt_dot(v_ref[:, cols(h)], head_of(do_all, h))
        dp_s[h] = dp
        st_lo[lo, HEADS + h : HEADS + h + 1, :] = jnp.sum(e_s[h] * dp, axis=0, keepdims=True) / totals[h]

    st = [
        remote(st_lo.at[lo], st_lo.at[lo], st_send.at[0, i], st_recv.at[0, lo], dev(z, a, b))
        for i, (a, b) in enumerate(lo_peers)
    ]
    loads[4].wait()
    loads[5].wait()
    row_of = lax.broadcasted_iota(jnp.int32, (16, HW), 0)
    col_of = lax.broadcasted_iota(jnp.int32, (16, HW), 1)
    diagonal = (col_of >= row_of * HD) & (col_of < (row_of + 1) * HD)
    nk_diag = jnp.where(diagonal, jnp.broadcast_to(nk_ref[...].astype(F32).reshape(1, HW), (16, HW)), 0.0).astype(BF16)
    nv_diag = jnp.where(diagonal, jnp.broadcast_to(nv_ref[...].astype(F32).reshape(1, HW), (16, HW)), 0.0).astype(BF16)
    whole_q = q_all[...].reshape(qt, HW)
    whole_do = do_all[...].reshape(qt, HW)
    null_score = (nt_dot(nk_diag, whole_q) * SCALE)[:HEADS]
    null_dp = nt_dot(nv_diag, whole_do)[:HEADS]

    def stat_arrived(stage, buf, at):
        pltpu.make_async_remote_copy(
            src_ref=buf.at[at], dst_ref=buf.at[at], send_sem=st_send.at[stage, 0], recv_sem=st_recv.at[stage, at],
            device_id=to_core, device_id_type=pl.DeviceIdType.MESH,
        ).wait_recv()

    for a, b in lo_peers:
        stat_arrived(0, st_lo, b * 2 + a)
    lse, delta = merge([st_lo[i, :HEADS] for i in range(4)], [st_lo[i, HEADS:] for i in range(4)])
    st_z[z, :HEADS, :] = lse
    st_z[z, HEADS:, :] = delta
    for j, o in enumerate(others_z):
        st.append(remote(st_z.at[z], st_z.at[z], st_send.at[1, j], st_recv.at[1, z], dev(o, y, core)))
    for o in others_z:
        stat_arrived(1, st_z, o)
    lse, delta = merge([st_z[i, :HEADS] for i in range(n_z)], [st_z[i, HEADS:] for i in range(n_z)])
    top = jnp.maximum(lse, null_score)
    log_total = top + jnp.log(jnp.exp(lse - top) + jnp.exp(null_score - top))
    null_prob = jnp.exp(null_score - log_total)
    delta = jnp.exp(lse - log_total) * delta + null_prob * null_dp
    null_ds = null_prob * (null_dp - delta)
    factor = jnp.exp(peak_s[:HEADS] - log_total)

    def dot(a, b):
        return jnp.dot(a, b, preferred_element_type=F32)

    rs = []
    far = pl.ds((1 - y) * n_z, n_z)
    near = pl.ds(y * n_z, n_z)

    def part_cols(part):
        return slice(part * WIDE, (part + 1) * WIDE)

    def dq_step(part):
        for i in range(PER):
            h = part * PER + i
            probs = e_s[h] * factor[h : h + 1]
            dscore = (probs * (dp_s[h] - delta[h : h + 1])).astype(BF16)
            p_s[h] = probs.astype(BF16)
            ds_s[h] = dscore
            dq = lax.dot_general(dscore, k_ref[:, cols(h)], TN, preferred_element_type=F32)
            dq = dq.reshape(2, 2 * n_z, rows, HD)
            dq_s[part, :, :, :, cols(i)] = dq
            dq_out[part, :, :, :, cols(i)] = dq.astype(BF16)
        rs.append(
            remote(dq_out.at[part, 1 - core], rs_c.at[part], rs_send.at[part, 0], rs_recv.at[part, 0], to_core)
        )

    def y_step(part):
        landed(rs_c.at[part], rs_send.at[part, 0], rs_recv.at[part, 0])
        y_out[part] = (dq_s[part, core, far] + rs_c[part, far].astype(F32)).astype(BF16)
        rs.append(remote(y_out.at[part], rs_y.at[part], rs_send.at[part, 1], rs_recv.at[part, 1], to_y))
        acc_s[part] = dq_s[part, core, near] + rs_c[part, near].astype(F32)

    def z_step(part):
        landed(rs_y.at[part], rs_send.at[part, 1], rs_recv.at[part, 1])
        acc = acc_s[part] + rs_y[part].astype(F32)
        acc_s[part] = acc
        z_out[part] = acc.astype(BF16)
        for j, o in enumerate(others_z):
            rs.append(
                remote(
                    z_out.at[part, o], rs_z.at[part, z], rs_send.at[part, 2 + j], rs_recv.at[part, 2 + z],
                    dev(o, y, core),
                )
            )

    def grad_v(h):
        gv_ref[:, cols(h)] = dot(p_s[h], head_of(do_all, h)).astype(BF16)

    def grad_k(h):
        gk_ref[:, cols(h)] = (dot(ds_s[h], head_of(q_all, h)) * SCALE).astype(BF16)

    dq_step(0)
    dq_step(1)
    y_step(0)
    dq_step(2)
    y_step(1)
    z_step(0)
    y_step(2)

    null_s[0, :HEADS, :] = null_ds
    null_s[1, :HEADS, :] = null_prob
    null_s[:, HEADS:, :] = jnp.zeros((2, 16 - HEADS, qt), F32)
    ds_high, ds_low = halves(null_s[0])
    p_high, p_low = halves(null_s[1])

    sum_k = dot(jnp.concatenate([ds_high, ds_low], axis=0), whole_q)
    sum_k = jnp.where(diagonal, sum_k[:16] + sum_k[16:], 0.0) * SCALE
    sum_v = dot(jnp.concatenate([p_high, p_low], axis=0), whole_do)
    sum_v = jnp.where(diagonal, sum_v[:16] + sum_v[16:], 0.0)
    null_sums[clip, 0:1, :] = jnp.sum(sum_k, axis=0, keepdims=True)
    null_sums[clip, 1:2, :] = jnp.sum(sum_v, axis=0, keepdims=True)
    ns = [
        remote(null_sums.at[clip], null_sums.at[clip], n_send.at[j], n_recv.at[clip], (o, bank))
        for j, o in enumerate(clip_peers)
    ]
    z_step(1)
    for h in range(HEADS // 2):
        grad_v(h)
    z_step(2)
    for h in range(HEADS // 2, HEADS):
        grad_v(h)
    stores = [pltpu.make_async_copy(gv_ref, gv_hbm, load_sem.at[6])]
    stores[0].start()

    own_at = lax.broadcasted_iota(jnp.int32, (rows, qt), 1) - mine * rows
    pick = (own_at == lax.broadcasted_iota(jnp.int32, (rows, qt), 0)).astype(F32).astype(BF16)
    own_high = nt_dot(pick, ds_high).astype(BF16)
    own_low = nt_dot(pick, ds_low).astype(BF16)
    null_term = dot(own_high, nk_diag) + dot(own_low, nk_diag)
    for h in range(HEADS):
        grad_k(h)
    stores.append(pltpu.make_async_copy(gk_ref, gk_hbm, load_sem.at[7]))
    stores[1].start()

    for part in range(PARTS):
        total = acc_s[part, z]
        for o in others_z:
            landed(rs_z.at[part, o], rs_send.at[part, 2], rs_recv.at[part, 2 + o])
            total = total + rs_z[part, o].astype(F32)
        gq_ref[:, part_cols(part)] = ((total + null_term[:, part_cols(part)]) * SCALE).astype(BF16)
    for o in clip_peers:
        landed(null_sums.at[o], n_send.at[0], n_recv.at[o])
    both = null_sums[0]
    for i in range(1, n_clip):
        both = both + null_sums[i]
    gnk_ref[...] = both[0]
    gnv_ref[...] = both[1]
    for copy in sends + st + rs + ns:
        copy.wait_send()
    for store in stores:
        store.wait()


def write_out(*refs):
    made, outs, sems = refs[:5], refs[5:10], refs[10]
    copies = [pltpu.make_async_copy(src, dst, sems.at[i]) for i, (src, dst) in enumerate(zip(made, outs))]
    for copy in copies:
        copy.start()
    for copy in copies:
        copy.wait()


def on_device(n_clip, n_bank, queries, keys, values, grad_out, null_key, null_value, bank_counts, block_slot):
    own_rows = queries.shape[1]
    rows = -(-own_rows // 16) * 16
    blk = keys.shape[1]
    q, do = queries[0], grad_out[0]
    if rows != own_rows:
        q = jnp.pad(q, ((0, rows - own_rows), (0, 0)))
        do = jnp.pad(do, ((0, rows - own_rows), (0, 0)))
    n_z = n_bank // 4
    qt = n_bank * rows
    vmem = pl.BlockSpec(memory_space=pltpu.VMEM)
    hbm = pl.BlockSpec(memory_space=pltpu.HBM)
    dma = pltpu.SemaphoreType.DMA
    shapes = (
        jax.ShapeDtypeStruct((rows, HW), BF16),
        jax.ShapeDtypeStruct((blk, HW), BF16),
        jax.ShapeDtypeStruct((blk, HW), BF16),
    )
    vector = jax.ShapeDtypeStruct((HW,), F32)
    made = pl.pallas_call(
        functools.partial(kernel, n_clip, n_z, rows, blk),
        out_shape=shapes + (vector, vector),
        in_specs=[pl.BlockSpec(memory_space=pltpu.SMEM)] * 2 + [hbm] * 6,
        out_specs=[vmem, hbm, hbm, vmem, vmem],
        scratch_shapes=[
            pltpu.VMEM((n_bank, rows, HW), BF16),
            pltpu.VMEM((n_bank, rows, HW), BF16),
            pltpu.VMEM((HEADS, blk, qt), F32),
            pltpu.VMEM((HEADS, blk, qt), F32),
            pltpu.VMEM((HEADS, blk, qt), BF16),
            pltpu.VMEM((HEADS, blk, qt), BF16),
            pltpu.VMEM((PARTS, 2, 2 * n_z, rows, WIDE), F32),
            pltpu.VMEM((PARTS, 2, 2 * n_z, rows, WIDE), BF16),
            pltpu.VMEM((PARTS, 2 * n_z, rows, WIDE), BF16),
            pltpu.VMEM((PARTS, n_z, rows, WIDE), BF16),
            pltpu.VMEM((PARTS, n_z, rows, WIDE), BF16),
            pltpu.VMEM((PARTS, n_z, rows, WIDE), F32),
            pltpu.VMEM((PARTS, n_z, rows, WIDE), BF16),
            pltpu.VMEM((PARTS, n_z, rows, WIDE), BF16),
            pltpu.VMEM((16, qt), F32),
            pltpu.VMEM((4, 2 * HEADS, qt), F32),
            pltpu.VMEM((n_z, 2 * HEADS, qt), F32),
            pltpu.VMEM((2, 16, qt), F32),
            pltpu.VMEM((n_clip, 2, HW), F32),
            pltpu.VMEM((blk, HW), BF16),
            pltpu.VMEM((blk, HW), BF16),
            pltpu.VMEM((HW,), BF16),
            pltpu.VMEM((HW,), BF16),
            pltpu.VMEM((blk, HW), BF16),
            pltpu.VMEM((blk, HW), BF16),
            dma((8,)),
            dma((2, n_bank)),
            dma((2, 2)),
            dma((2, n_z)),
            dma((2, n_z)),
            dma((2, 2)),
            dma((2, max(4, n_z))),
            dma((2, max(4, n_z))),
            dma((PARTS, 2 + n_z)),
            dma((PARTS, 2 + n_z)),
            dma((n_clip,)),
            dma((n_clip,)),
        ],
        compiler_params=pltpu.CompilerParams(
            collective_id=0, has_side_effects=True, vmem_limit_bytes=58 * 1024 * 1024
        ),
    )(bank_counts, block_slot, q, keys[0], values[0], do, null_key, null_value)
    gq, gk, gv, gnk, gnv = pl.pallas_call(
        write_out,
        out_shape=shapes + (vector, vector),
        in_specs=[hbm] * 5,
        out_specs=[hbm] * 5,
        scratch_shapes=[dma((5,))],
        compiler_params=pltpu.CompilerParams(vmem_limit_bytes=60 * 1024 * 1024),
    )(*made)
    return gq[None, :own_rows], gk[None], gv[None], gnk, gnv


def solution(mesh):
    return jax.shard_map(
        functools.partial(on_device, mesh.shape["clip"], mesh.shape["bank"]),
        mesh=mesh,
        in_specs=(
            P("clip", "bank", None),
            P("clip", "bank", None),
            P("clip", "bank", None),
            P("clip", "bank", None),
            P(),
            P(),
            P("clip"),
            P("clip", "bank"),
        ),
        out_specs=(
            P("clip", "bank", None),
            P("clip", "bank", None),
            P("clip", "bank", None),
            P(),
            P(),
        ),
        check_vma=False,
    )
```

```python
import functools

import jax
import jax.numpy as jnp
from jax import lax
from jax.experimental import pallas as pl
from jax.experimental.pallas import tpu as pltpu
from jax.sharding import PartitionSpec as P

HEADS = 12
HD = 128
HW = HEADS * HD
SCALE = HD ** (-0.5)
F32 = jnp.float32
BF16 = jnp.bfloat16
PARTS = 3
PER = HEADS // PARTS
WIDE = PER * HD
NT = (((1,), (1,)), ((), ()))
TN = (((0,), (0,)), ((), ()))


def nt_dot(a, b):
    return lax.dot_general(a, b, NT, preferred_element_type=F32)


def halves(x):
    high = x.astype(BF16)
    return high, (x - high.astype(F32)).astype(BF16)


def merge(lses, deltas):
    top = functools.reduce(jnp.maximum, lses)
    weights = [jnp.exp(one - top) for one in lses]
    total = sum(weights[1:], weights[0])
    mixed = weights[0] * deltas[0]
    for weight, delta in zip(weights[1:], deltas[1:]):
        mixed = mixed + weight * delta
    return top + jnp.log(total), mixed / total


def kernel(
    n_clip, n_z, rows, blk,
    count_ref, slot_ref, q_hbm, k_hbm, v_hbm, do_hbm, nk_hbm, nv_hbm,
    gq_ref, gk_hbm, gv_hbm, gnk_ref, gnv_ref,
    q_all, do_all, e_s, dp_s, p_s, ds_s, dq_s, dq_out, rs_c, y_out, rs_y, acc_s, z_out, rs_z,
    peak_s, st_lo, st_z, null_s, null_sums,
    k_ref, v_ref, nk_ref, nv_ref, gk_ref, gv_ref, load_sem,
    g_recv, g_recv_c, g_send_z, g_send_y, g_send_c, st_send, st_recv, rs_send, rs_recv, n_send, n_recv,
):
    n = 4 * n_z
    qt = n * rows
    clip = lax.axis_index("clip")
    bank = lax.axis_index("bank")
    core = lax.rem(bank, 2)
    y = lax.rem(bank // 2, 2)
    z = bank // 4

    def dev(z_, y_, c_):
        return (clip, (z_ * 2 + y_) * 2 + c_)

    def place(z_, y_, c_):
        return (c_ * 2 + y_) * n_z + z_

    mine = place(z, y, core)
    others_z = [lax.rem(z + j, n_z) for j in range(1, n_z)]
    lo_peers = [(y, 1 - core), (1 - y, core), (1 - y, 1 - core)]
    to_core, to_y = dev(z, y, 1 - core), dev(z, 1 - y, core)
    clip_peers = [lax.rem(clip + j, n_clip) for j in range(1, n_clip)]

    loads = [
        pltpu.make_async_copy(src, dst, load_sem.at[i])
        for i, (src, dst) in enumerate(
            [
                (q_hbm, q_all.at[mine]), (do_hbm, do_all.at[mine]), (k_hbm, k_ref), (v_hbm, v_ref),
                (nk_hbm, nk_ref), (nv_hbm, nv_ref),
            ]
        )
    ]
    for load in loads:
        load.start()

    barrier = pltpu.get_barrier_semaphore()
    peers = [dev(z, a, b) for a, b in lo_peers] + [dev(o, y, core) for o in others_z]
    peers += [(o, bank) for o in clip_peers]
    for peer in peers:
        pl.semaphore_signal(barrier, inc=1, device_id=peer, device_id_type=pl.DeviceIdType.MESH)
    pl.semaphore_wait(barrier, len(peers))

    def remote(src, dst, send, recv, device):
        copy = pltpu.make_async_remote_copy(
            src_ref=src, dst_ref=dst, send_sem=send, recv_sem=recv,
            device_id=device, device_id_type=pl.DeviceIdType.MESH,
        )
        copy.start()
        return copy

    gathered = (q_all, do_all)
    sends = []

    def own_sends(a):
        own = gathered[a].at[mine]
        for j, o in enumerate(others_z):
            sends.append(remote(own, own, g_send_z.at[a, j], g_recv.at[a, mine], dev(o, y, core)))
        sends.append(remote(own, own, g_send_y.at[a, 0], g_recv.at[a, mine], to_y))

    def landed(buf, send, recv):
        pltpu.make_async_remote_copy(
            src_ref=buf, dst_ref=buf, send_sem=send, recv_sem=recv,
            device_id=to_core, device_id_type=pl.DeviceIdType.MESH,
        ).wait_recv()

    def slab(a, y_, c_):
        return gathered[a].at[pl.ds(place(0, y_, c_), n_z)]

    def to_other_core(a, y_):
        here = slab(a, y_, core)
        sends.append(remote(here, here, g_send_c.at[a, y_], g_recv_c.at[a, y_], to_core))

    def forward(a, step):
        if step < n_z - 1:
            at = place(others_z[step], y, core)
            here = gathered[a].at[at]
            landed(here, g_send_z.at[a, 0], g_recv.at[a, at])
            sends.append(remote(here, here, g_send_y.at[a, step + 1], g_recv.at[a, at], to_y))
            if step == n_z - 2:
                to_other_core(a, y)
        else:
            at = place(([z] + others_z)[step - (n_z - 1)], 1 - y, core)
            landed(gathered[a].at[at], g_send_z.at[a, 0], g_recv.at[a, at])
            if step == 2 * n_z - 2:
                to_other_core(a, 1 - y)

    def from_core(a):
        for y_ in (y, 1 - y):
            landed(slab(a, y_, 1 - core), g_send_c.at[a, 0], g_recv_c.at[a, y_])

    loads[0].wait()
    own_sends(0)
    loads[1].wait()
    steps = 2 * n_z - 1
    for step in range(n_z - 1):
        forward(0, step)
    own_sends(1)
    for step in range(n_z - 1, steps):
        forward(0, step)
    loads[2].wait()
    from_core(0)

    live = lax.broadcasted_iota(jnp.int32, (blk, qt), 0) < count_ref[0] - slot_ref[0, 0] * blk
    lo = core * 2 + y

    def cols(h):
        return slice(h * HD, (h + 1) * HD)

    def head_of(ref, h):
        return ref[:, :, cols(h)].reshape(qt, HD)

    totals = []
    done = 0
    for h in range(HEADS):
        until = min(steps, (steps * max(h - 1, 0) + 8) // 9)
        for step in range(done, until):
            forward(1, step)
        done = max(done, until)
        scores = nt_dot(k_ref[:, cols(h)], head_of(q_all, h)) * SCALE
        scores = jnp.where(live, scores, -1e30)
        peak = jnp.max(scores, axis=0, keepdims=True)
        e = jnp.exp(scores - peak)
        total = jnp.sum(e, axis=0, keepdims=True)
        e_s[h] = e
        peak_s[h : h + 1, :] = peak
        st_lo[lo, h : h + 1, :] = peak + jnp.log(total)
        totals.append(total)
    for step in range(done, steps):
        forward(1, step)
    loads[3].wait()
    from_core(1)
    for h in range(HEADS):
        dp = nt_dot(v_ref[:, cols(h)], head_of(do_all, h))
        dp_s[h] = dp
        st_lo[lo, HEADS + h : HEADS + h + 1, :] = jnp.sum(e_s[h] * dp, axis=0, keepdims=True) / totals[h]

    st = [
        remote(st_lo.at[lo], st_lo.at[lo], st_send.at[0, i], st_recv.at[0, lo], dev(z, a, b))
        for i, (a, b) in enumerate(lo_peers)
    ]
    loads[4].wait()
    loads[5].wait()
    row_of = lax.broadcasted_iota(jnp.int32, (16, HW), 0)
    col_of = lax.broadcasted_iota(jnp.int32, (16, HW), 1)
    diagonal = (col_of >= row_of * HD) & (col_of < (row_of + 1) * HD)
    nk_diag = jnp.where(diagonal, jnp.broadcast_to(nk_ref[...].astype(F32).reshape(1, HW), (16, HW)), 0.0).astype(BF16)
    nv_diag = jnp.where(diagonal, jnp.broadcast_to(nv_ref[...].astype(F32).reshape(1, HW), (16, HW)), 0.0).astype(BF16)
    whole_q = q_all[...].reshape(qt, HW)
    whole_do = do_all[...].reshape(qt, HW)
    null_score = (nt_dot(nk_diag, whole_q) * SCALE)[:HEADS]
    null_dp = nt_dot(nv_diag, whole_do)[:HEADS]

    def stat_arrived(stage, buf, at):
        pltpu.make_async_remote_copy(
            src_ref=buf.at[at], dst_ref=buf.at[at], send_sem=st_send.at[stage, 0], recv_sem=st_recv.at[stage, at],
            device_id=to_core, device_id_type=pl.DeviceIdType.MESH,
        ).wait_recv()

    for a, b in lo_peers:
        stat_arrived(0, st_lo, b * 2 + a)
    lse, delta = merge([st_lo[i, :HEADS] for i in range(4)], [st_lo[i, HEADS:] for i in range(4)])
    st_z[z, :HEADS, :] = lse
    st_z[z, HEADS:, :] = delta
    for j, o in enumerate(others_z):
        st.append(remote(st_z.at[z], st_z.at[z], st_send.at[1, j], st_recv.at[1, z], dev(o, y, core)))
    for o in others_z:
        stat_arrived(1, st_z, o)
    lse, delta = merge([st_z[i, :HEADS] for i in range(n_z)], [st_z[i, HEADS:] for i in range(n_z)])
    top = jnp.maximum(lse, null_score)
    log_total = top + jnp.log(jnp.exp(lse - top) + jnp.exp(null_score - top))
    null_prob = jnp.exp(null_score - log_total)
    delta = jnp.exp(lse - log_total) * delta + null_prob * null_dp
    null_ds = null_prob * (null_dp - delta)
    factor = jnp.exp(peak_s[:HEADS] - log_total)

    def dot(a, b):
        return jnp.dot(a, b, preferred_element_type=F32)

    rs = []
    far = pl.ds((1 - y) * n_z, n_z)
    near = pl.ds(y * n_z, n_z)

    def part_cols(part):
        return slice(part * WIDE, (part + 1) * WIDE)

    def dq_step(part):
        for i in range(PER):
            h = part * PER + i
            probs = e_s[h] * factor[h : h + 1]
            dscore = (probs * (dp_s[h] - delta[h : h + 1])).astype(BF16)
            p_s[h] = probs.astype(BF16)
            ds_s[h] = dscore
            dq = lax.dot_general(dscore, k_ref[:, cols(h)], TN, preferred_element_type=F32)
            dq = dq.reshape(2, 2 * n_z, rows, HD)
            dq_s[part, :, :, :, cols(i)] = dq
            dq_out[part, :, :, :, cols(i)] = dq.astype(BF16)
        rs.append(
            remote(dq_out.at[part, 1 - core], rs_c.at[part], rs_send.at[part, 0], rs_recv.at[part, 0], to_core)
        )

    def y_step(part):
        landed(rs_c.at[part], rs_send.at[part, 0], rs_recv.at[part, 0])
        y_out[part] = (dq_s[part, core, far] + rs_c[part, far].astype(F32)).astype(BF16)
        rs.append(remote(y_out.at[part], rs_y.at[part], rs_send.at[part, 1], rs_recv.at[part, 1], to_y))
        acc_s[part] = dq_s[part, core, near] + rs_c[part, near].astype(F32)

    def z_step(part):
        landed(rs_y.at[part], rs_send.at[part, 1], rs_recv.at[part, 1])
        acc = acc_s[part] + rs_y[part].astype(F32)
        acc_s[part] = acc
        z_out[part] = acc.astype(BF16)
        for j, o in enumerate(others_z):
            rs.append(
                remote(
                    z_out.at[part, o], rs_z.at[part, z], rs_send.at[part, 2 + j], rs_recv.at[part, 2 + z],
                    dev(o, y, core),
                )
            )

    def grad_v(h):
        gv_ref[:, cols(h)] = dot(p_s[h], head_of(do_all, h)).astype(BF16)

    def grad_k(h):
        gk_ref[:, cols(h)] = (dot(ds_s[h], head_of(q_all, h)) * SCALE).astype(BF16)

    dq_step(0)
    dq_step(1)
    y_step(0)
    dq_step(2)
    y_step(1)
    z_step(0)
    y_step(2)

    null_s[0, :HEADS, :] = null_ds
    null_s[1, :HEADS, :] = null_prob
    null_s[:, HEADS:, :] = jnp.zeros((2, 16 - HEADS, qt), F32)
    ds_high, ds_low = halves(null_s[0])
    p_high, p_low = halves(null_s[1])

    sum_k = dot(jnp.concatenate([ds_high, ds_low], axis=0), whole_q)
    sum_k = jnp.where(diagonal, sum_k[:16] + sum_k[16:], 0.0) * SCALE
    sum_v = dot(jnp.concatenate([p_high, p_low], axis=0), whole_do)
    sum_v = jnp.where(diagonal, sum_v[:16] + sum_v[16:], 0.0)
    null_sums[clip, 0:1, :] = jnp.sum(sum_k, axis=0, keepdims=True)
    null_sums[clip, 1:2, :] = jnp.sum(sum_v, axis=0, keepdims=True)
    ns = [
        remote(null_sums.at[clip], null_sums.at[clip], n_send.at[j], n_recv.at[clip], (o, bank))
        for j, o in enumerate(clip_peers)
    ]
    z_step(1)
    for h in range(HEADS // 2):
        grad_v(h)
    z_step(2)
    for h in range(HEADS // 2, HEADS):
        grad_v(h)
    stores = [pltpu.make_async_copy(gv_ref, gv_hbm, load_sem.at[6])]
    stores[0].start()

    own_at = lax.broadcasted_iota(jnp.int32, (rows, qt), 1) - mine * rows
    pick = (own_at == lax.broadcasted_iota(jnp.int32, (rows, qt), 0)).astype(F32).astype(BF16)
    own_high = nt_dot(pick, ds_high).astype(BF16)
    own_low = nt_dot(pick, ds_low).astype(BF16)
    null_term = dot(own_high, nk_diag) + dot(own_low, nk_diag)
    for h in range(HEADS):
        grad_k(h)
    stores.append(pltpu.make_async_copy(gk_ref, gk_hbm, load_sem.at[7]))
    stores[1].start()

    for part in range(PARTS):
        total = acc_s[part, z]
        for o in others_z:
            landed(rs_z.at[part, o], rs_send.at[part, 2], rs_recv.at[part, 2 + o])
            total = total + rs_z[part, o].astype(F32)
        gq_ref[:, part_cols(part)] = ((total + null_term[:, part_cols(part)]) * SCALE).astype(BF16)
    for o in clip_peers:
        landed(null_sums.at[o], n_send.at[0], n_recv.at[o])
    both = null_sums[0]
    for i in range(1, n_clip):
        both = both + null_sums[i]
    gnk_ref[...] = both[0]
    gnv_ref[...] = both[1]
    for copy in sends + st + rs + ns:
        copy.wait_send()
    for store in stores:
        store.wait()


def write_out(*refs):
    made, outs, held, load_sems, store_sems = refs[:5], refs[5:10], refs[10:15], refs[15], refs[16]
    loads = [pltpu.make_async_copy(src, at, load_sems.at[i]) for i, (src, at) in enumerate(zip(made, held))]
    stores = [pltpu.make_async_copy(at, dst, store_sems.at[i]) for i, (at, dst) in enumerate(zip(held, outs))]
    for load in loads:
        load.start()
    for load, store in zip(loads, stores):
        load.wait()
        store.start()
    for store in stores:
        store.wait()


def on_device(n_clip, n_bank, queries, keys, values, grad_out, null_key, null_value, bank_counts, block_slot):
    own_rows = queries.shape[1]
    rows = -(-own_rows // 16) * 16
    blk = keys.shape[1]
    q, do = queries[0], grad_out[0]
    if rows != own_rows:
        q = jnp.pad(q, ((0, rows - own_rows), (0, 0)))
        do = jnp.pad(do, ((0, rows - own_rows), (0, 0)))
    n_z = n_bank // 4
    qt = n_bank * rows
    vmem = pl.BlockSpec(memory_space=pltpu.VMEM)
    hbm = pl.BlockSpec(memory_space=pltpu.HBM)
    dma = pltpu.SemaphoreType.DMA
    shapes = (
        jax.ShapeDtypeStruct((rows, HW), BF16),
        jax.ShapeDtypeStruct((blk, HW), BF16),
        jax.ShapeDtypeStruct((blk, HW), BF16),
    )
    vector = jax.ShapeDtypeStruct((HW,), F32)
    made = pl.pallas_call(
        functools.partial(kernel, n_clip, n_z, rows, blk),
        out_shape=shapes + (vector, vector),
        in_specs=[pl.BlockSpec(memory_space=pltpu.SMEM)] * 2 + [hbm] * 6,
        out_specs=[vmem, hbm, hbm, vmem, vmem],
        scratch_shapes=[
            pltpu.VMEM((n_bank, rows, HW), BF16),
            pltpu.VMEM((n_bank, rows, HW), BF16),
            pltpu.VMEM((HEADS, blk, qt), F32),
            pltpu.VMEM((HEADS, blk, qt), F32),
            pltpu.VMEM((HEADS, blk, qt), BF16),
            pltpu.VMEM((HEADS, blk, qt), BF16),
            pltpu.VMEM((PARTS, 2, 2 * n_z, rows, WIDE), F32),
            pltpu.VMEM((PARTS, 2, 2 * n_z, rows, WIDE), BF16),
            pltpu.VMEM((PARTS, 2 * n_z, rows, WIDE), BF16),
            pltpu.VMEM((PARTS, n_z, rows, WIDE), BF16),
            pltpu.VMEM((PARTS, n_z, rows, WIDE), BF16),
            pltpu.VMEM((PARTS, n_z, rows, WIDE), F32),
            pltpu.VMEM((PARTS, n_z, rows, WIDE), BF16),
            pltpu.VMEM((PARTS, n_z, rows, WIDE), BF16),
            pltpu.VMEM((16, qt), F32),
            pltpu.VMEM((4, 2 * HEADS, qt), F32),
            pltpu.VMEM((n_z, 2 * HEADS, qt), F32),
            pltpu.VMEM((2, 16, qt), F32),
            pltpu.VMEM((n_clip, 2, HW), F32),
            pltpu.VMEM((blk, HW), BF16),
            pltpu.VMEM((blk, HW), BF16),
            pltpu.VMEM((HW,), BF16),
            pltpu.VMEM((HW,), BF16),
            pltpu.VMEM((blk, HW), BF16),
            pltpu.VMEM((blk, HW), BF16),
            dma((8,)),
            dma((2, n_bank)),
            dma((2, 2)),
            dma((2, n_z)),
            dma((2, n_z)),
            dma((2, 2)),
            dma((2, max(4, n_z))),
            dma((2, max(4, n_z))),
            dma((PARTS, 2 + n_z)),
            dma((PARTS, 2 + n_z)),
            dma((n_clip,)),
            dma((n_clip,)),
        ],
        compiler_params=pltpu.CompilerParams(
            collective_id=0, has_side_effects=True, vmem_limit_bytes=58 * 1024 * 1024
        ),
    )(bank_counts, block_slot, q, keys[0], values[0], do, null_key, null_value)
    gq, gk, gv, gnk, gnv = pl.pallas_call(
        write_out,
        out_shape=shapes + (vector, vector),
        in_specs=[hbm] * 5,
        out_specs=[hbm] * 5,
        scratch_shapes=[pltpu.VMEM(one.shape, one.dtype) for one in shapes + (vector, vector)] + [dma((5,)), dma((5,))],
        compiler_params=pltpu.CompilerParams(vmem_limit_bytes=60 * 1024 * 1024),
    )(*made)
    return gq[None, :own_rows], gk[None], gv[None], gnk, gnv


def solution(mesh):
    return jax.shard_map(
        functools.partial(on_device, mesh.shape["clip"], mesh.shape["bank"]),
        mesh=mesh,
        in_specs=(
            P("clip", "bank", None),
            P("clip", "bank", None),
            P("clip", "bank", None),
            P("clip", "bank", None),
            P(),
            P(),
            P("clip"),
            P("clip", "bank"),
        ),
        out_specs=(
            P("clip", "bank", None),
            P("clip", "bank", None),
            P("clip", "bank", None),
            P(),
            P(),
        ),
        check_vma=False,
    )
```

```python
import functools

import jax
import jax.numpy as jnp
from jax import lax
from jax.experimental import pallas as pl
from jax.experimental.pallas import tpu as pltpu
from jax.sharding import PartitionSpec as P

HEADS = 12
HD = 128
HW = HEADS * HD
SCALE = HD ** (-0.5)
F32 = jnp.float32
BF16 = jnp.bfloat16
PARTS = 3
PER = HEADS // PARTS
WIDE = PER * HD
NT = (((1,), (1,)), ((), ()))
TN = (((0,), (0,)), ((), ()))


def nt_dot(a, b):
    return lax.dot_general(a, b, NT, preferred_element_type=F32)


def halves(x):
    high = x.astype(BF16)
    return high, (x - high.astype(F32)).astype(BF16)


def merge(lses, deltas):
    top = functools.reduce(jnp.maximum, lses)
    weights = [jnp.exp(one - top) for one in lses]
    total = sum(weights[1:], weights[0])
    mixed = weights[0] * deltas[0]
    for weight, delta in zip(weights[1:], deltas[1:]):
        mixed = mixed + weight * delta
    return top + jnp.log(total), mixed / total


def kernel(
    n_clip, n_z, rows, blk,
    count_ref, slot_ref, q_hbm, k_hbm, v_hbm, do_hbm, nk_hbm, nv_hbm,
    gq_ref, gk_hbm, gv_hbm, gnk_ref, gnv_ref,
    q_all, do_all, e_s, dp_s, p_s, ds_s, dq_s, dq_out, rs_c, y_out, rs_y, acc_s, z_out, rs_z,
    peak_s, st_lo, st_z, null_s, null_sums,
    k_ref, v_ref, nk_ref, nv_ref, gk_ref, gv_ref, load_sem,
    g_recv, g_recv_c, g_send_z, g_send_y, g_send_c, st_send, st_recv, rs_send, rs_recv, n_send, n_recv,
):
    n = 4 * n_z
    qt = n * rows
    clip = lax.axis_index("clip")
    bank = lax.axis_index("bank")
    core = lax.rem(bank, 2)
    y = lax.rem(bank // 2, 2)
    z = bank // 4

    def dev(z_, y_, c_):
        return (clip, (z_ * 2 + y_) * 2 + c_)

    def place(z_, y_, c_):
        return (c_ * 2 + y_) * n_z + z_

    mine = place(z, y, core)
    others_z = [lax.rem(z + j, n_z) for j in range(1, n_z)]
    lo_peers = [(y, 1 - core), (1 - y, core), (1 - y, 1 - core)]
    to_core, to_y = dev(z, y, 1 - core), dev(z, 1 - y, core)
    clip_peers = [lax.rem(clip + j, n_clip) for j in range(1, n_clip)]

    loads = [
        pltpu.make_async_copy(src, dst, load_sem.at[i])
        for i, (src, dst) in enumerate(
            [
                (q_hbm, q_all.at[mine]), (do_hbm, do_all.at[mine]), (k_hbm, k_ref), (v_hbm, v_ref),
                (nk_hbm, nk_ref), (nv_hbm, nv_ref),
            ]
        )
    ]
    for load in loads:
        load.start()

    barrier = pltpu.get_barrier_semaphore()
    peers = [dev(z, a, b) for a, b in lo_peers] + [dev(o, y, core) for o in others_z]
    peers += [(o, bank) for o in clip_peers]
    for peer in peers:
        pl.semaphore_signal(barrier, inc=1, device_id=peer, device_id_type=pl.DeviceIdType.MESH)
    pl.semaphore_wait(barrier, len(peers))

    def remote(src, dst, send, recv, device):
        copy = pltpu.make_async_remote_copy(
            src_ref=src, dst_ref=dst, send_sem=send, recv_sem=recv,
            device_id=device, device_id_type=pl.DeviceIdType.MESH,
        )
        copy.start()
        return copy

    gathered = (q_all, do_all)
    sends = []

    def own_sends(a):
        own = gathered[a].at[mine]
        for j, o in enumerate(others_z):
            sends.append(remote(own, own, g_send_z.at[a, j], g_recv.at[a, mine], dev(o, y, core)))
        sends.append(remote(own, own, g_send_y.at[a, 0], g_recv.at[a, mine], to_y))

    def landed(buf, send, recv):
        pltpu.make_async_remote_copy(
            src_ref=buf, dst_ref=buf, send_sem=send, recv_sem=recv,
            device_id=to_core, device_id_type=pl.DeviceIdType.MESH,
        ).wait_recv()

    def slab(a, y_, c_):
        return gathered[a].at[pl.ds(place(0, y_, c_), n_z)]

    def to_other_core(a, y_):
        here = slab(a, y_, core)
        sends.append(remote(here, here, g_send_c.at[a, y_], g_recv_c.at[a, y_], to_core))

    def forward(a, step):
        if step < n_z - 1:
            at = place(others_z[step], y, core)
            here = gathered[a].at[at]
            landed(here, g_send_z.at[a, 0], g_recv.at[a, at])
            sends.append(remote(here, here, g_send_y.at[a, step + 1], g_recv.at[a, at], to_y))
            if step == n_z - 2:
                to_other_core(a, y)
        else:
            at = place(([z] + others_z)[step - (n_z - 1)], 1 - y, core)
            landed(gathered[a].at[at], g_send_z.at[a, 0], g_recv.at[a, at])
            if step == 2 * n_z - 2:
                to_other_core(a, 1 - y)

    def from_core(a):
        for y_ in (y, 1 - y):
            landed(slab(a, y_, 1 - core), g_send_c.at[a, 0], g_recv_c.at[a, y_])

    loads[0].wait()
    own_sends(0)
    loads[1].wait()
    steps = 2 * n_z - 1
    for step in range(n_z - 1):
        forward(0, step)
    own_sends(1)
    for step in range(n_z - 1, steps):
        forward(0, step)
    loads[2].wait()
    from_core(0)

    live = lax.broadcasted_iota(jnp.int32, (blk, qt), 0) < count_ref[0] - slot_ref[0, 0] * blk
    lo = core * 2 + y

    def cols(h):
        return slice(h * HD, (h + 1) * HD)

    def head_of(ref, h):
        return ref[:, :, cols(h)].reshape(qt, HD)

    totals = []
    done = 0
    for h in range(HEADS):
        until = min(steps, (steps * max(h - 1, 0) + 8) // 9)
        for step in range(done, until):
            forward(1, step)
        done = max(done, until)
        scores = nt_dot(k_ref[:, cols(h)], head_of(q_all, h)) * SCALE
        scores = jnp.where(live, scores, -1e30)
        peak = jnp.max(scores, axis=0, keepdims=True)
        e = jnp.exp(scores - peak)
        total = jnp.sum(e, axis=0, keepdims=True)
        e_s[h] = e
        peak_s[h : h + 1, :] = peak
        st_lo[h // PER, lo, h % PER : h % PER + 1, :] = peak + jnp.log(total)
        totals.append(total)
    for step in range(done, steps):
        forward(1, step)
    loads[3].wait()
    from_core(1)
    st = []

    def delta_part(part):
        for i in range(PER):
            h = part * PER + i
            dp = nt_dot(v_ref[:, cols(h)], head_of(do_all, h))
            dp_s[h] = dp
            delta = jnp.sum(e_s[h] * dp, axis=0, keepdims=True) / totals[h]
            st_lo[part, lo, PER + i : PER + i + 1, :] = delta
        own = st_lo.at[part, lo]
        for i, (a, b) in enumerate(lo_peers):
            st.append(remote(own, own, st_send.at[part, i], st_recv.at[part, lo], dev(z, a, b)))

    def merged(buf, part, count):
        return merge([buf[part, i, :PER] for i in range(count)], [buf[part, i, PER:] for i in range(count)])

    def spread_part(part):
        for a, b in lo_peers:
            at = b * 2 + a
            landed(st_lo.at[part, at], st_send.at[part, 0], st_recv.at[part, at])
        lse, delta = merged(st_lo, part, 4)
        st_z[part, z, :PER, :] = lse
        st_z[part, z, PER:, :] = delta
        own = st_z.at[part, z]
        for j, o in enumerate(others_z):
            st.append(
                remote(own, own, st_send.at[PARTS + part, j], st_recv.at[PARTS + part, z], dev(o, y, core))
            )

    delta_part(0)
    delta_part(1)
    spread_part(0)
    delta_part(2)
    spread_part(1)
    loads[4].wait()
    loads[5].wait()
    row_of = lax.broadcasted_iota(jnp.int32, (16, HW), 0)
    col_of = lax.broadcasted_iota(jnp.int32, (16, HW), 1)
    diagonal = (col_of >= row_of * HD) & (col_of < (row_of + 1) * HD)
    nk_diag = jnp.where(diagonal, jnp.broadcast_to(nk_ref[...].astype(F32).reshape(1, HW), (16, HW)), 0.0).astype(BF16)
    nv_diag = jnp.where(diagonal, jnp.broadcast_to(nv_ref[...].astype(F32).reshape(1, HW), (16, HW)), 0.0).astype(BF16)
    whole_q = q_all[...].reshape(qt, HW)
    whole_do = do_all[...].reshape(qt, HW)
    null_score = (nt_dot(nk_diag, whole_q) * SCALE)[:HEADS]
    null_dp = nt_dot(nv_diag, whole_do)[:HEADS]
    spread_part(2)

    def final_part(part):
        for o in others_z:
            landed(st_z.at[part, o], st_send.at[PARTS + part, 0], st_recv.at[PARTS + part, o])
        lse, delta = merged(st_z, part, n_z)
        at = slice(part * PER, (part + 1) * PER)
        score, null_d = null_score[at], null_dp[at]
        top = jnp.maximum(lse, score)
        log_total = top + jnp.log(jnp.exp(lse - top) + jnp.exp(score - top))
        null_prob = jnp.exp(score - log_total)
        delta = jnp.exp(lse - log_total) * delta + null_prob * null_d
        null_s[0, at, :] = null_prob * (null_d - delta)
        null_s[1, at, :] = null_prob
        return jnp.exp(peak_s[at] - log_total), delta

    def dot(a, b):
        return jnp.dot(a, b, preferred_element_type=F32)

    rs = []
    far = pl.ds((1 - y) * n_z, n_z)
    near = pl.ds(y * n_z, n_z)

    def part_cols(part):
        return slice(part * WIDE, (part + 1) * WIDE)

    def dq_step(part):
        factor, delta = final_part(part)
        for i in range(PER):
            h = part * PER + i
            probs = e_s[h] * factor[i : i + 1]
            dscore = (probs * (dp_s[h] - delta[i : i + 1])).astype(BF16)
            p_s[h] = probs.astype(BF16)
            ds_s[h] = dscore
            dq = lax.dot_general(dscore, k_ref[:, cols(h)], TN, preferred_element_type=F32)
            dq = dq.reshape(2, 2 * n_z, rows, HD)
            dq_s[part, :, :, :, cols(i)] = dq
            dq_out[part, :, :, :, cols(i)] = dq.astype(BF16)
        rs.append(
            remote(dq_out.at[part, 1 - core], rs_c.at[part], rs_send.at[part, 0], rs_recv.at[part, 0], to_core)
        )

    def y_step(part):
        landed(rs_c.at[part], rs_send.at[part, 0], rs_recv.at[part, 0])
        y_out[part] = (dq_s[part, core, far] + rs_c[part, far].astype(F32)).astype(BF16)
        rs.append(remote(y_out.at[part], rs_y.at[part], rs_send.at[part, 1], rs_recv.at[part, 1], to_y))
        acc_s[part] = dq_s[part, core, near] + rs_c[part, near].astype(F32)

    def z_step(part):
        landed(rs_y.at[part], rs_send.at[part, 1], rs_recv.at[part, 1])
        acc = acc_s[part] + rs_y[part].astype(F32)
        acc_s[part] = acc
        z_out[part] = acc.astype(BF16)
        for j, o in enumerate(others_z):
            rs.append(
                remote(
                    z_out.at[part, o], rs_z.at[part, z], rs_send.at[part, 2 + j], rs_recv.at[part, 2 + z],
                    dev(o, y, core),
                )
            )

    def grad_v(h):
        gv_ref[:, cols(h)] = dot(p_s[h], head_of(do_all, h)).astype(BF16)

    def grad_k(h):
        gk_ref[:, cols(h)] = (dot(ds_s[h], head_of(q_all, h)) * SCALE).astype(BF16)

    dq_step(0)
    dq_step(1)
    y_step(0)
    dq_step(2)
    y_step(1)
    z_step(0)
    y_step(2)

    null_s[:, HEADS:, :] = jnp.zeros((2, 16 - HEADS, qt), F32)
    ds_high, ds_low = halves(null_s[0])
    p_high, p_low = halves(null_s[1])

    sum_k = dot(jnp.concatenate([ds_high, ds_low], axis=0), whole_q)
    sum_k = jnp.where(diagonal, sum_k[:16] + sum_k[16:], 0.0) * SCALE
    sum_v = dot(jnp.concatenate([p_high, p_low], axis=0), whole_do)
    sum_v = jnp.where(diagonal, sum_v[:16] + sum_v[16:], 0.0)
    null_sums[clip, 0:1, :] = jnp.sum(sum_k, axis=0, keepdims=True)
    null_sums[clip, 1:2, :] = jnp.sum(sum_v, axis=0, keepdims=True)
    ns = [
        remote(null_sums.at[clip], null_sums.at[clip], n_send.at[j], n_recv.at[clip], (o, bank))
        for j, o in enumerate(clip_peers)
    ]
    z_step(1)
    for h in range(HEADS // 2):
        grad_v(h)
    z_step(2)
    for h in range(HEADS // 2, HEADS):
        grad_v(h)
    stores = [pltpu.make_async_copy(gv_ref, gv_hbm, load_sem.at[6])]
    stores[0].start()

    own_at = lax.broadcasted_iota(jnp.int32, (rows, qt), 1) - mine * rows
    pick = (own_at == lax.broadcasted_iota(jnp.int32, (rows, qt), 0)).astype(F32).astype(BF16)
    own_high = nt_dot(pick, ds_high).astype(BF16)
    own_low = nt_dot(pick, ds_low).astype(BF16)
    null_term = dot(own_high, nk_diag) + dot(own_low, nk_diag)
    for h in range(HEADS):
        grad_k(h)
    stores.append(pltpu.make_async_copy(gk_ref, gk_hbm, load_sem.at[7]))
    stores[1].start()

    for part in range(PARTS):
        total = acc_s[part, z]
        for o in others_z:
            landed(rs_z.at[part, o], rs_send.at[part, 2], rs_recv.at[part, 2 + o])
            total = total + rs_z[part, o].astype(F32)
        gq_ref[:, part_cols(part)] = ((total + null_term[:, part_cols(part)]) * SCALE).astype(BF16)
    for o in clip_peers:
        landed(null_sums.at[o], n_send.at[0], n_recv.at[o])
    both = null_sums[0]
    for i in range(1, n_clip):
        both = both + null_sums[i]
    gnk_ref[...] = both[0]
    gnv_ref[...] = both[1]
    for copy in sends + st + rs + ns:
        copy.wait_send()
    for store in stores:
        store.wait()


def write_out(*refs):
    made, outs, held, load_sems, store_sems = refs[:5], refs[5:10], refs[10:15], refs[15], refs[16]
    loads = [pltpu.make_async_copy(src, at, load_sems.at[i]) for i, (src, at) in enumerate(zip(made, held))]
    stores = [pltpu.make_async_copy(at, dst, store_sems.at[i]) for i, (at, dst) in enumerate(zip(held, outs))]
    for load in loads:
        load.start()
    for load, store in zip(loads, stores):
        load.wait()
        store.start()
    for store in stores:
        store.wait()


def on_device(n_clip, n_bank, queries, keys, values, grad_out, null_key, null_value, bank_counts, block_slot):
    own_rows = queries.shape[1]
    rows = -(-own_rows // 16) * 16
    blk = keys.shape[1]
    q, do = queries[0], grad_out[0]
    if rows != own_rows:
        q = jnp.pad(q, ((0, rows - own_rows), (0, 0)))
        do = jnp.pad(do, ((0, rows - own_rows), (0, 0)))
    n_z = n_bank // 4
    qt = n_bank * rows
    vmem = pl.BlockSpec(memory_space=pltpu.VMEM)
    hbm = pl.BlockSpec(memory_space=pltpu.HBM)
    dma = pltpu.SemaphoreType.DMA
    shapes = (
        jax.ShapeDtypeStruct((rows, HW), BF16),
        jax.ShapeDtypeStruct((blk, HW), BF16),
        jax.ShapeDtypeStruct((blk, HW), BF16),
    )
    vector = jax.ShapeDtypeStruct((HW,), F32)
    made = pl.pallas_call(
        functools.partial(kernel, n_clip, n_z, rows, blk),
        out_shape=shapes + (vector, vector),
        in_specs=[pl.BlockSpec(memory_space=pltpu.SMEM)] * 2 + [hbm] * 6,
        out_specs=[vmem, hbm, hbm, vmem, vmem],
        scratch_shapes=[
            pltpu.VMEM((n_bank, rows, HW), BF16),
            pltpu.VMEM((n_bank, rows, HW), BF16),
            pltpu.VMEM((HEADS, blk, qt), F32),
            pltpu.VMEM((HEADS, blk, qt), F32),
            pltpu.VMEM((HEADS, blk, qt), BF16),
            pltpu.VMEM((HEADS, blk, qt), BF16),
            pltpu.VMEM((PARTS, 2, 2 * n_z, rows, WIDE), F32),
            pltpu.VMEM((PARTS, 2, 2 * n_z, rows, WIDE), BF16),
            pltpu.VMEM((PARTS, 2 * n_z, rows, WIDE), BF16),
            pltpu.VMEM((PARTS, n_z, rows, WIDE), BF16),
            pltpu.VMEM((PARTS, n_z, rows, WIDE), BF16),
            pltpu.VMEM((PARTS, n_z, rows, WIDE), F32),
            pltpu.VMEM((PARTS, n_z, rows, WIDE), BF16),
            pltpu.VMEM((PARTS, n_z, rows, WIDE), BF16),
            pltpu.VMEM((16, qt), F32),
            pltpu.VMEM((PARTS, 4, 2 * PER, qt), F32),
            pltpu.VMEM((PARTS, n_z, 2 * PER, qt), F32),
            pltpu.VMEM((2, 16, qt), F32),
            pltpu.VMEM((n_clip, 2, HW), F32),
            pltpu.VMEM((blk, HW), BF16),
            pltpu.VMEM((blk, HW), BF16),
            pltpu.VMEM((HW,), BF16),
            pltpu.VMEM((HW,), BF16),
            pltpu.VMEM((blk, HW), BF16),
            pltpu.VMEM((blk, HW), BF16),
            dma((8,)),
            dma((2, n_bank)),
            dma((2, 2)),
            dma((2, n_z)),
            dma((2, n_z)),
            dma((2, 2)),
            dma((2 * PARTS, max(4, n_z))),
            dma((2 * PARTS, max(4, n_z))),
            dma((PARTS, 2 + n_z)),
            dma((PARTS, 2 + n_z)),
            dma((n_clip,)),
            dma((n_clip,)),
        ],
        compiler_params=pltpu.CompilerParams(
            collective_id=0, has_side_effects=True, vmem_limit_bytes=58 * 1024 * 1024
        ),
    )(bank_counts, block_slot, q, keys[0], values[0], do, null_key, null_value)
    gq, gk, gv, gnk, gnv = pl.pallas_call(
        write_out,
        out_shape=shapes + (vector, vector),
        in_specs=[hbm] * 5,
        out_specs=[hbm] * 5,
        scratch_shapes=[pltpu.VMEM(one.shape, one.dtype) for one in shapes + (vector, vector)] + [dma((5,)), dma((5,))],
        compiler_params=pltpu.CompilerParams(vmem_limit_bytes=60 * 1024 * 1024),
    )(*made)
    return gq[None, :own_rows], gk[None], gv[None], gnk, gnv


def solution(mesh):
    return jax.shard_map(
        functools.partial(on_device, mesh.shape["clip"], mesh.shape["bank"]),
        mesh=mesh,
        in_specs=(
            P("clip", "bank", None),
            P("clip", "bank", None),
            P("clip", "bank", None),
            P("clip", "bank", None),
            P(),
            P(),
            P("clip"),
            P("clip", "bank"),
        ),
        out_specs=(
            P("clip", "bank", None),
            P("clip", "bank", None),
            P("clip", "bank", None),
            P(),
            P(),
        ),
        check_vma=False,
    )
```

```python
import functools

import jax
import jax.numpy as jnp
from jax import lax
from jax.experimental import pallas as pl
from jax.experimental.pallas import tpu as pltpu
from jax.sharding import PartitionSpec as P

HEADS = 12
HD = 128
HW = HEADS * HD
SCALE = HD ** (-0.5)
F32 = jnp.float32
BF16 = jnp.bfloat16
PARTS = 3
PER = HEADS // PARTS
WIDE = PER * HD
NT = (((1,), (1,)), ((), ()))
TN = (((0,), (0,)), ((), ()))


def nt_dot(a, b):
    return lax.dot_general(a, b, NT, preferred_element_type=F32)


def halves(x):
    high = x.astype(BF16)
    return high, (x - high.astype(F32)).astype(BF16)


def merge(lses, deltas):
    top = functools.reduce(jnp.maximum, lses)
    weights = [jnp.exp(one - top) for one in lses]
    total = sum(weights[1:], weights[0])
    mixed = weights[0] * deltas[0]
    for weight, delta in zip(weights[1:], deltas[1:]):
        mixed = mixed + weight * delta
    return top + jnp.log(total), mixed / total


def kernel(
    n_clip, n_z, rows, blk,
    count_ref, slot_ref, q_hbm, k_hbm, v_hbm, do_hbm, nk_hbm, nv_hbm,
    gq_ref, gk_hbm, gv_hbm, gnk_ref, gnv_ref,
    q_all, do_all, e_s, dp_s, p_s, ds_s, dq_s, dq_out, rs_c, y_out, rs_y, acc_s, z_out, rs_z,
    peak_s, st_lo, st_z, null_s, null_sums,
    k_ref, v_ref, nk_ref, nv_ref, gk_ref, gv_ref, load_sem,
    g_recv, g_recv_c, g_send_z, g_send_y, g_send_c, st_send, st_recv, rs_send, rs_recv, n_send, n_recv,
):
    n = 4 * n_z
    qt = n * rows
    clip = lax.axis_index("clip")
    bank = lax.axis_index("bank")
    core = lax.rem(bank, 2)
    y = lax.rem(bank // 2, 2)
    z = bank // 4

    def dev(z_, y_, c_):
        return (clip, (z_ * 2 + y_) * 2 + c_)

    def place(z_, y_, c_):
        return (c_ * 2 + y_) * n_z + z_

    mine = place(z, y, core)
    others_z = [lax.rem(z + j, n_z) for j in range(1, n_z)]
    lo_peers = [(y, 1 - core), (1 - y, core), (1 - y, 1 - core)]
    to_core, to_y = dev(z, y, 1 - core), dev(z, 1 - y, core)
    clip_peers = [lax.rem(clip + j, n_clip) for j in range(1, n_clip)]

    loads = [
        pltpu.make_async_copy(src, dst, load_sem.at[i])
        for i, (src, dst) in enumerate(
            [
                (q_hbm, q_all.at[mine]), (do_hbm, do_all.at[mine]), (k_hbm, k_ref), (v_hbm, v_ref),
                (nk_hbm, nk_ref), (nv_hbm, nv_ref),
            ]
        )
    ]
    for load in loads:
        load.start()

    barrier = pltpu.get_barrier_semaphore()
    peers = [dev(z, a, b) for a, b in lo_peers] + [dev(o, y, core) for o in others_z]
    peers += [(o, bank) for o in clip_peers]
    for peer in peers:
        pl.semaphore_signal(barrier, inc=1, device_id=peer, device_id_type=pl.DeviceIdType.MESH)
    pl.semaphore_wait(barrier, len(peers))

    def remote(src, dst, send, recv, device):
        copy = pltpu.make_async_remote_copy(
            src_ref=src, dst_ref=dst, send_sem=send, recv_sem=recv,
            device_id=device, device_id_type=pl.DeviceIdType.MESH,
        )
        copy.start()
        return copy

    gathered = (q_all, do_all)
    sends = []

    def own_sends(a):
        own = gathered[a].at[mine]
        sends.append(remote(own, own, g_send_y.at[a, 0], g_recv.at[a, mine], to_y))
        for j, o in enumerate(others_z):
            sends.append(remote(own, own, g_send_z.at[a, j], g_recv.at[a, mine], dev(o, y, core)))

    def landed(buf, send, recv):
        pltpu.make_async_remote_copy(
            src_ref=buf, dst_ref=buf, send_sem=send, recv_sem=recv,
            device_id=to_core, device_id_type=pl.DeviceIdType.MESH,
        ).wait_recv()

    def slab(a, y_, c_):
        return gathered[a].at[pl.ds(place(0, y_, c_), n_z)]

    def to_other_core(a, y_):
        here = slab(a, y_, core)
        sends.append(remote(here, here, g_send_c.at[a, y_], g_recv_c.at[a, y_], to_core))

    def forward(a, step):
        if step < n_z - 1:
            at = place(others_z[step], y, core)
            here = gathered[a].at[at]
            landed(here, g_send_z.at[a, 0], g_recv.at[a, at])
            sends.append(remote(here, here, g_send_y.at[a, step + 1], g_recv.at[a, at], to_y))
            if step == n_z - 2:
                to_other_core(a, y)
        else:
            at = place(([z] + others_z)[step - (n_z - 1)], 1 - y, core)
            landed(gathered[a].at[at], g_send_z.at[a, 0], g_recv.at[a, at])
            if step == 2 * n_z - 2:
                to_other_core(a, 1 - y)

    def from_core(a):
        for y_ in (y, 1 - y):
            landed(slab(a, y_, 1 - core), g_send_c.at[a, 0], g_recv_c.at[a, y_])

    loads[0].wait()
    own_sends(0)
    loads[1].wait()
    steps = 2 * n_z - 1
    for step in range(n_z - 1):
        forward(0, step)
    own_sends(1)
    for step in range(n_z - 1, steps):
        forward(0, step)
    loads[2].wait()
    from_core(0)

    live = lax.broadcasted_iota(jnp.int32, (blk, qt), 0) < count_ref[0] - slot_ref[0, 0] * blk
    lo = core * 2 + y

    def cols(h):
        return slice(h * HD, (h + 1) * HD)

    def head_of(ref, h):
        return ref[:, :, cols(h)].reshape(qt, HD)

    totals = []
    done = 0
    for h in range(HEADS):
        until = min(steps, (steps * max(h - 1, 0) + 8) // 9)
        for step in range(done, until):
            forward(1, step)
        done = max(done, until)
        scores = nt_dot(k_ref[:, cols(h)], head_of(q_all, h)) * SCALE
        scores = jnp.where(live, scores, -1e30)
        peak = jnp.max(scores, axis=0, keepdims=True)
        e = jnp.exp(scores - peak)
        total = jnp.sum(e, axis=0, keepdims=True)
        e_s[h] = e
        peak_s[h : h + 1, :] = peak
        st_lo[h // PER, lo, h % PER : h % PER + 1, :] = peak + jnp.log(total)
        totals.append(total)
    for step in range(done, steps):
        forward(1, step)
    loads[3].wait()
    from_core(1)
    st = []

    def delta_part(part):
        for i in range(PER):
            h = part * PER + i
            dp = nt_dot(v_ref[:, cols(h)], head_of(do_all, h))
            dp_s[h] = dp
            delta = jnp.sum(e_s[h] * dp, axis=0, keepdims=True) / totals[h]
            st_lo[part, lo, PER + i : PER + i + 1, :] = delta
        own = st_lo.at[part, lo]
        for i, (a, b) in enumerate(lo_peers):
            st.append(remote(own, own, st_send.at[part, i], st_recv.at[part, lo], dev(z, a, b)))

    def merged(buf, part, count):
        return merge([buf[part, i, :PER] for i in range(count)], [buf[part, i, PER:] for i in range(count)])

    def spread_part(part):
        for a, b in lo_peers:
            at = b * 2 + a
            landed(st_lo.at[part, at], st_send.at[part, 0], st_recv.at[part, at])
        lse, delta = merged(st_lo, part, 4)
        st_z[part, z, :PER, :] = lse
        st_z[part, z, PER:, :] = delta
        own = st_z.at[part, z]
        for j, o in enumerate(others_z):
            st.append(
                remote(own, own, st_send.at[PARTS + part, j], st_recv.at[PARTS + part, z], dev(o, y, core))
            )

    delta_part(0)
    delta_part(1)
    spread_part(0)
    delta_part(2)
    spread_part(1)
    loads[4].wait()
    loads[5].wait()
    row_of = lax.broadcasted_iota(jnp.int32, (16, HW), 0)
    col_of = lax.broadcasted_iota(jnp.int32, (16, HW), 1)
    diagonal = (col_of >= row_of * HD) & (col_of < (row_of + 1) * HD)
    nk_diag = jnp.where(diagonal, jnp.broadcast_to(nk_ref[...].astype(F32).reshape(1, HW), (16, HW)), 0.0).astype(BF16)
    nv_diag = jnp.where(diagonal, jnp.broadcast_to(nv_ref[...].astype(F32).reshape(1, HW), (16, HW)), 0.0).astype(BF16)
    whole_q = q_all[...].reshape(qt, HW)
    whole_do = do_all[...].reshape(qt, HW)
    null_score = (nt_dot(nk_diag, whole_q) * SCALE)[:HEADS]
    null_dp = nt_dot(nv_diag, whole_do)[:HEADS]
    spread_part(2)

    def final_part(part):
        for o in others_z:
            landed(st_z.at[part, o], st_send.at[PARTS + part, 0], st_recv.at[PARTS + part, o])
        lse, delta = merged(st_z, part, n_z)
        at = slice(part * PER, (part + 1) * PER)
        score, null_d = null_score[at], null_dp[at]
        top = jnp.maximum(lse, score)
        log_total = top + jnp.log(jnp.exp(lse - top) + jnp.exp(score - top))
        null_prob = jnp.exp(score - log_total)
        delta = jnp.exp(lse - log_total) * delta + null_prob * null_d
        null_s[0, at, :] = null_prob * (null_d - delta)
        null_s[1, at, :] = null_prob
        return jnp.exp(peak_s[at] - log_total), delta

    def dot(a, b):
        return jnp.dot(a, b, preferred_element_type=F32)

    rs = []
    far = pl.ds((1 - y) * n_z, n_z)
    near = pl.ds(y * n_z, n_z)

    def part_cols(part):
        return slice(part * WIDE, (part + 1) * WIDE)

    def dq_step(part):
        factor, delta = final_part(part)
        for i in range(PER):
            h = part * PER + i
            probs = e_s[h] * factor[i : i + 1]
            dscore = (probs * (dp_s[h] - delta[i : i + 1])).astype(BF16)
            p_s[h] = probs.astype(BF16)
            ds_s[h] = dscore
            dq = lax.dot_general(dscore, k_ref[:, cols(h)], TN, preferred_element_type=F32)
            dq = dq.reshape(2, 2 * n_z, rows, HD)
            dq_s[part, :, :, :, cols(i)] = dq
            dq_out[part, :, :, :, cols(i)] = dq.astype(BF16)
        rs.append(
            remote(dq_out.at[part, 1 - core], rs_c.at[part], rs_send.at[part, 0], rs_recv.at[part, 0], to_core)
        )

    def y_step(part):
        landed(rs_c.at[part], rs_send.at[part, 0], rs_recv.at[part, 0])
        y_out[part] = (dq_s[part, core, far] + rs_c[part, far].astype(F32)).astype(BF16)
        rs.append(remote(y_out.at[part], rs_y.at[part], rs_send.at[part, 1], rs_recv.at[part, 1], to_y))
        acc_s[part] = dq_s[part, core, near] + rs_c[part, near].astype(F32)

    def z_step(part):
        landed(rs_y.at[part], rs_send.at[part, 1], rs_recv.at[part, 1])
        acc = acc_s[part] + rs_y[part].astype(F32)
        acc_s[part] = acc
        z_out[part] = acc.astype(BF16)
        for j, o in enumerate(others_z):
            rs.append(
                remote(
                    z_out.at[part, o], rs_z.at[part, z], rs_send.at[part, 2 + j], rs_recv.at[part, 2 + z],
                    dev(o, y, core),
                )
            )

    def grad_v(h):
        gv_ref[:, cols(h)] = dot(p_s[h], head_of(do_all, h)).astype(BF16)

    def grad_k(h):
        gk_ref[:, cols(h)] = (dot(ds_s[h], head_of(q_all, h)) * SCALE).astype(BF16)

    dq_step(0)
    dq_step(1)
    y_step(0)
    dq_step(2)
    y_step(1)
    z_step(0)
    y_step(2)

    null_s[:, HEADS:, :] = jnp.zeros((2, 16 - HEADS, qt), F32)
    ds_high, ds_low = halves(null_s[0])
    p_high, p_low = halves(null_s[1])

    sum_k = dot(jnp.concatenate([ds_high, ds_low], axis=0), whole_q)
    sum_k = jnp.where(diagonal, sum_k[:16] + sum_k[16:], 0.0) * SCALE
    sum_v = dot(jnp.concatenate([p_high, p_low], axis=0), whole_do)
    sum_v = jnp.where(diagonal, sum_v[:16] + sum_v[16:], 0.0)
    null_sums[clip, 0:1, :] = jnp.sum(sum_k, axis=0, keepdims=True)
    null_sums[clip, 1:2, :] = jnp.sum(sum_v, axis=0, keepdims=True)
    ns = [
        remote(null_sums.at[clip], null_sums.at[clip], n_send.at[j], n_recv.at[clip], (o, bank))
        for j, o in enumerate(clip_peers)
    ]
    z_step(1)
    for h in range(HEADS // 2):
        grad_v(h)
    z_step(2)
    for h in range(HEADS // 2, HEADS):
        grad_v(h)
    stores = [pltpu.make_async_copy(gv_ref, gv_hbm, load_sem.at[6])]
    stores[0].start()

    own_at = lax.broadcasted_iota(jnp.int32, (rows, qt), 1) - mine * rows
    pick = (own_at == lax.broadcasted_iota(jnp.int32, (rows, qt), 0)).astype(F32).astype(BF16)
    own_high = nt_dot(pick, ds_high).astype(BF16)
    own_low = nt_dot(pick, ds_low).astype(BF16)
    null_term = dot(own_high, nk_diag) + dot(own_low, nk_diag)
    for h in range(HEADS):
        grad_k(h)
    stores.append(pltpu.make_async_copy(gk_ref, gk_hbm, load_sem.at[7]))
    stores[1].start()

    for part in range(PARTS):
        total = acc_s[part, z]
        for o in others_z:
            landed(rs_z.at[part, o], rs_send.at[part, 2], rs_recv.at[part, 2 + o])
            total = total + rs_z[part, o].astype(F32)
        gq_ref[:, part_cols(part)] = ((total + null_term[:, part_cols(part)]) * SCALE).astype(BF16)
    for o in clip_peers:
        landed(null_sums.at[o], n_send.at[0], n_recv.at[o])
    both = null_sums[0]
    for i in range(1, n_clip):
        both = both + null_sums[i]
    gnk_ref[...] = both[0]
    gnv_ref[...] = both[1]
    for copy in sends + st + rs + ns:
        copy.wait_send()
    for store in stores:
        store.wait()


def write_out(*refs):
    made, outs, held, load_sems, store_sems = refs[:5], refs[5:10], refs[10:15], refs[15], refs[16]
    loads = [pltpu.make_async_copy(src, at, load_sems.at[i]) for i, (src, at) in enumerate(zip(made, held))]
    stores = [pltpu.make_async_copy(at, dst, store_sems.at[i]) for i, (at, dst) in enumerate(zip(held, outs))]
    for load in loads:
        load.start()
    for load, store in zip(loads, stores):
        load.wait()
        store.start()
    for store in stores:
        store.wait()


def on_device(n_clip, n_bank, queries, keys, values, grad_out, null_key, null_value, bank_counts, block_slot):
    own_rows = queries.shape[1]
    rows = -(-own_rows // 16) * 16
    blk = keys.shape[1]
    q, do = queries[0], grad_out[0]
    if rows != own_rows:
        q = jnp.pad(q, ((0, rows - own_rows), (0, 0)))
        do = jnp.pad(do, ((0, rows - own_rows), (0, 0)))
    n_z = n_bank // 4
    qt = n_bank * rows
    vmem = pl.BlockSpec(memory_space=pltpu.VMEM)
    hbm = pl.BlockSpec(memory_space=pltpu.HBM)
    dma = pltpu.SemaphoreType.DMA
    shapes = (
        jax.ShapeDtypeStruct((rows, HW), BF16),
        jax.ShapeDtypeStruct((blk, HW), BF16),
        jax.ShapeDtypeStruct((blk, HW), BF16),
    )
    vector = jax.ShapeDtypeStruct((HW,), F32)
    made = pl.pallas_call(
        functools.partial(kernel, n_clip, n_z, rows, blk),
        out_shape=shapes + (vector, vector),
        in_specs=[pl.BlockSpec(memory_space=pltpu.SMEM)] * 2 + [hbm] * 6,
        out_specs=[vmem, hbm, hbm, vmem, vmem],
        scratch_shapes=[
            pltpu.VMEM((n_bank, rows, HW), BF16),
            pltpu.VMEM((n_bank, rows, HW), BF16),
            pltpu.VMEM((HEADS, blk, qt), F32),
            pltpu.VMEM((HEADS, blk, qt), F32),
            pltpu.VMEM((HEADS, blk, qt), BF16),
            pltpu.VMEM((HEADS, blk, qt), BF16),
            pltpu.VMEM((PARTS, 2, 2 * n_z, rows, WIDE), F32),
            pltpu.VMEM((PARTS, 2, 2 * n_z, rows, WIDE), BF16),
            pltpu.VMEM((PARTS, 2 * n_z, rows, WIDE), BF16),
            pltpu.VMEM((PARTS, n_z, rows, WIDE), BF16),
            pltpu.VMEM((PARTS, n_z, rows, WIDE), BF16),
            pltpu.VMEM((PARTS, n_z, rows, WIDE), F32),
            pltpu.VMEM((PARTS, n_z, rows, WIDE), BF16),
            pltpu.VMEM((PARTS, n_z, rows, WIDE), BF16),
            pltpu.VMEM((16, qt), F32),
            pltpu.VMEM((PARTS, 4, 2 * PER, qt), F32),
            pltpu.VMEM((PARTS, n_z, 2 * PER, qt), F32),
            pltpu.VMEM((2, 16, qt), F32),
            pltpu.VMEM((n_clip, 2, HW), F32),
            pltpu.VMEM((blk, HW), BF16),
            pltpu.VMEM((blk, HW), BF16),
            pltpu.VMEM((HW,), BF16),
            pltpu.VMEM((HW,), BF16),
            pltpu.VMEM((blk, HW), BF16),
            pltpu.VMEM((blk, HW), BF16),
            dma((8,)),
            dma((2, n_bank)),
            dma((2, 2)),
            dma((2, n_z)),
            dma((2, n_z)),
            dma((2, 2)),
            dma((2 * PARTS, max(4, n_z))),
            dma((2 * PARTS, max(4, n_z))),
            dma((PARTS, 2 + n_z)),
            dma((PARTS, 2 + n_z)),
            dma((n_clip,)),
            dma((n_clip,)),
        ],
        compiler_params=pltpu.CompilerParams(
            collective_id=0, has_side_effects=True, vmem_limit_bytes=58 * 1024 * 1024
        ),
    )(bank_counts, block_slot, q, keys[0], values[0], do, null_key, null_value)
    gq, gk, gv, gnk, gnv = pl.pallas_call(
        write_out,
        out_shape=shapes + (vector, vector),
        in_specs=[hbm] * 5,
        out_specs=[hbm] * 5,
        scratch_shapes=[pltpu.VMEM(one.shape, one.dtype) for one in shapes + (vector, vector)] + [dma((5,)), dma((5,))],
        compiler_params=pltpu.CompilerParams(vmem_limit_bytes=60 * 1024 * 1024),
    )(*made)
    return gq[None, :own_rows], gk[None], gv[None], gnk, gnv


def solution(mesh):
    return jax.shard_map(
        functools.partial(on_device, mesh.shape["clip"], mesh.shape["bank"]),
        mesh=mesh,
        in_specs=(
            P("clip", "bank", None),
            P("clip", "bank", None),
            P("clip", "bank", None),
            P("clip", "bank", None),
            P(),
            P(),
            P("clip"),
            P("clip", "bank"),
        ),
        out_specs=(
            P("clip", "bank", None),
            P("clip", "bank", None),
            P("clip", "bank", None),
            P(),
            P(),
        ),
        check_vma=False,
    )
```
